256 devices in a mesh: row: 8 (over y, core), col: 32 (over z, x).
Axes of the slice: x: 4, y: 4, z: 8, core: 2. Of those that a mesh axis runs over, the one named last changes fastest.
Arguments:
- source: bfloat16 [16384, 512], P('row'), may hold values from -16 to 16
- target: bfloat16 [16384, 512], P('col'), may hold values from -6 to 6
- log_source_mass: float32 [16384], P('row'), may hold values from -1.5 to 1.5
- log_target_mass: float32 [16384], P('col'), may hold values from -1.5 to 1.5
Outputs:
- source_image: float32 [16384, 512], P(('row', 'col'))
- target_image: float32 [16384, 512], P('col')
The draws below stay inside these ranges and needn't reach their ends.
All inputs are finite; a program needn't handle non-finite values.
Results may differ from the reference program's by a relative error of at most 0.0055.
Values sent between devices are 32-bit elements; how exact they have to be, the bound alone decides.
A program may use at most 64 MiB of HBM per device.

```python
import jax
import jax.numpy as jnp
from jax import lax

D = 512
S_DEV = 2048
ITERS = 2
NS = 16384
NT = 16384
N_ROW = 8


def draw_source(key, part):
    key = jax.random.fold_in(key, 11)
    first = jax.random.fold_in(key, 0)
    base = jax.random.normal(first, (NS, D), jnp.float32)
    return jnp.clip(base, -16.0, 16.0).astype(jnp.bfloat16)


def block_levels(stream_key, shape, shards, least, high):
    gain, own = 1.0, jax.random.fold_in(stream_key, 6)
    for dim, blocks in shards:
        heights = jnp.exp(jax.random.uniform(jax.random.fold_in(own, dim), (blocks,), jnp.float32, least / len(shards), high / len(shards)))
        gain = gain * jnp.repeat(heights, shape[dim] // blocks).reshape([-1 if axis == dim else 1 for axis in range(len(shape))])
    return gain


def bell_draw(key, dims, deviation, most, shards=(), held_as=jnp.bfloat16):
    entries = jax.random.normal(key, dims, jnp.float32) * deviation
    if len(shards) > 0:
        entries = block_levels(key, dims, shards, -0.22, 0.18) * entries
    return jnp.clip(entries, min=-most, max=most).astype(held_as)


def setup_inputs(seed: int = 0) -> dict:
    key_list = jax.random.split(jax.random.key(seed), 5)
    source = draw_source(jax.random.fold_in(key_list[4], 71), 0)
    target = bell_draw(key_list[1], (NT, D), 1.0, 6.0, ((0, 32),))
    log_source_mass = jnp.clip(jax.random.uniform(key_list[2], (NS,), jnp.float32, -1.5, 1.5) * block_levels(key_list[2], (NS,), ((0, 8),), -0.4, 0.0), -1.5, 1.5)
    log_target_mass = jnp.clip(jax.random.uniform(key_list[3], (NT,), jnp.float32, -1.5, 1.5) * block_levels(key_list[3], (NT,), ((0, 32),), -0.4, 0.0), -1.5, 1.5)
    return dict(source=source, target=target, log_source_mass=log_source_mass, log_target_mass=log_target_mass)


blur = 0.1


def block_cost(xb, sqx, yall, sqy):
    inner = jnp.dot(xb.astype(jnp.float32), yall.astype(jnp.float32).T, precision=lax.Precision.HIGHEST)
    return (sqx[:, None] + sqy[None, :] - 2.0 * inner) / D


def reference(source, target, log_source_mass, log_target_mass):
    sqx_all = jnp.sum(source.astype(jnp.float32) ** 2, axis=1)
    sqy = jnp.sum(target.astype(jnp.float32) ** 2, axis=1)
    xs = source.reshape(N_ROW, S_DEV, D)
    sqxs = sqx_all.reshape(N_ROW, S_DEV)
    las = log_source_mass.reshape(N_ROW, S_DEV)
    g = jnp.zeros((NT,), jnp.float32)
    f = jnp.zeros((NS,), jnp.float32)
    for step in range(ITERS):
        def row_pass(item):
            xb, sqb = item
            scores = log_target_mass[None, :] + (g[None, :] - block_cost(xb, sqb, target, sqy)) / blur
            peak = jnp.max(scores, axis=1)
            return -blur * (peak + jnp.log(jnp.sum(jnp.exp(scores - peak[:, None]), axis=1)))
        f = lax.map(row_pass, (xs, sqxs)).reshape(NS)
        fs = f.reshape(N_ROW, S_DEV)

        def col_pass(carry, item):
            peak, total = carry
            xb, sqb, fb, lab = item
            scores = lab[:, None] + (fb[:, None] - block_cost(xb, sqb, target, sqy)) / blur
            local = jnp.max(scores, axis=0)
            top = jnp.maximum(peak, local)
            total = total * jnp.exp(peak - top) + jnp.sum(jnp.exp(scores - top[None, :]), axis=0)
            return (top, total), None
        init = (jnp.full((NT,), -jnp.inf, jnp.float32), jnp.zeros((NT,), jnp.float32))
        (peak, total), unused = lax.scan(col_pass, init, (xs, sqxs, fs, las))
        g = -blur * (peak + jnp.log(total))
    fs = f.reshape(N_ROW, S_DEV)

    def final_pass(carry, item):
        numer, denom = carry
        xb, sqb, fb, lab = item
        plan = jnp.exp(lab[:, None] + log_target_mass[None, :] + (fb[:, None] + g[None, :] - block_cost(xb, sqb, target, sqy)) / blur)
        weights = plan.astype(jnp.bfloat16).astype(jnp.float32)
        src = jnp.dot(weights, target.astype(jnp.float32), precision=lax.Precision.HIGHEST) / jnp.sum(plan, axis=1)[:, None]
        numer = numer + jnp.dot(weights.T, xb.astype(jnp.float32), precision=lax.Precision.HIGHEST)
        denom = denom + jnp.sum(plan, axis=0)
        return (numer, denom), src
    init = (jnp.zeros((NT, D), jnp.float32), jnp.zeros((NT,), jnp.float32))
    (numer, denom), src = lax.scan(final_pass, init, (xs, sqxs, fs, las))
    return src.reshape(NS, D), numer / denom[:, None]
```

```python
import functools
import math

import jax
import jax.numpy as jnp
from jax import lax
from jax.experimental import pallas as pl
from jax.experimental.pallas import tpu as pltpu
from jax.sharding import PartitionSpec as P

D = 512
NI = 2048
NJ = 512
NY, NK, NZ, NX = 4, 2, 8, 4
OWN = NI // (NZ * NX)
HALF = NJ // NK
QUART = HALF // NY
BLUR = 0.1
LOG2E = math.log2(math.e)
NORM = LOG2E / (D * BLUR)
MESH = pl.DeviceIdType.MESH
F32 = jnp.float32
BF16 = jnp.bfloat16

X_PEERS = [1, 2, 3]
Y_PEERS = [2, 1, 3]
Z_PEERS = [4, 3, 5, 2, 6, 1, 7]
ROW_PEERS = [(dy, dk) for dy in (2, 1, 3, 0) for dk in (1, 0) if (dy, dk) != (0, 0)]
WIDE_PEERS = [
    (dy, dk, dx) for dy in (2, 1, 3, 0) for dx in (2, 1, 3, 0) for dk in (1, 0) if (dy, dk, dx) != (0, 0, 0)
]


def log2(x):
    return jnp.log(x) * LOG2E


def merge(parts):
    peak = functools.reduce(jnp.maximum, parts)
    return peak + log2(sum(jnp.exp2(part - peak) for part in parts))


def merge_rows(x):
    peak = jnp.max(x, axis=0, keepdims=True)
    return peak + log2(jnp.sum(jnp.exp2(x - peak), axis=0, keepdims=True))


def to_column(row):
    return jnp.broadcast_to(row, (128, row.shape[1])).T


def nt_dot(a, b):
    return lax.dot_general(a, b, (((1,), (1,)), ((), ())), preferred_element_type=F32)


def squared_norms(x):
    sq = x.astype(F32)
    sq = sq * sq
    high = sq.astype(BF16)
    low = (sq - high.astype(F32)).astype(BF16)
    ones = jnp.ones((8, D), BF16)
    return (nt_dot(ones, high) + nt_dot(ones, low))[:1]


def kernel(
    src, tgt, lsm, ltm, simg, timg,
    xt, x2, t4, tf, trecv, own, fparts, gparts, acol, browb, num, dparts,
    aux, auxr, lf, lfx, lfz, lg, lgr, lgw, bcol,
    tn, tsib, tc, ty, tout, plus, minus, dn, dnr,
    pf_s, pf_r, sib_s, sib_r, aux_s, aux_r, fx_s, fx_r, fz_s, fz_r, gr_s, gr_r, gw_s, gw_r,
    ts_s, ts_r, ty_s, ty_r, ta_s, ta_r, tb_s, tb_r, plus_s, plus_r, minus_s, minus_r, dn_s, dn_r,
):
    row, col = lax.axis_index("row"), lax.axis_index("col")
    y, k, z, x = row // NK, row % NK, col // NX, col % NX

    def dev(dy=0, dk=0, dz=0, dx=0):
        return {
            "row": lax.rem(y + dy, NY) * NK + lax.rem(k + dk, NK),
            "col": lax.rem(z + dz, NZ) * NX + lax.rem(x + dx, NX),
        }

    def send(source, target, send_sem, recv_sem, **to):
        copy = pltpu.make_async_remote_copy(
            source, target, send_sem, recv_sem, device_id=dev(**to), device_id_type=MESH
        )
        copy.start()

    def wait(ref, sem):
        pltpu.make_async_copy(ref, ref, sem).wait()

    barrier = pltpu.get_barrier_semaphore()
    for dy, dk, dx in WIDE_PEERS:
        pl.semaphore_signal(barrier, 1, device_id=dev(dy, dk, 0, dx), device_id_type=MESH)
    for dz in Z_PEERS:
        pl.semaphore_signal(barrier, 1, device_id=dev(dz=dz), device_id_type=MESH)

    tf[...] = tgt[...].astype(F32)
    t4[:NJ, :] = tgt[...]
    ls2 = lsm[...] * LOG2E
    lt2 = ltm[...] * LOG2E
    sqy = squared_norms(tgt[...]) * NORM
    aux[0:1, :] = lt2
    aux[1:2, :] = sqy
    acol[...] = to_column(lt2 - sqy)
    pl.semaphore_wait(barrier, len(WIDE_PEERS) + len(Z_PEERS))
    half = pl.ds(pl.multiple_of(k * HALF, HALF), HALF)
    other = pl.ds(pl.multiple_of((1 - k) * HALF, HALF), HALF)
    for dx in X_PEERS:
        send(aux, auxr.at[dx - 1], aux_s, aux_r, dx=dx)
    for dx in X_PEERS:
        send(tf.at[half], trecv.at[dx - 1, half], pf_s, pf_r.at[dx - 1], dx=dx)

    for c in range(NI // 256):
        xt[:, c * 256 : (c + 1) * 256] = nt_dot(tgt[...], src[c * 256 : (c + 1) * 256, :]) * (2 * NORM)

    def f_local(out):
        def tile(t, carry):
            lanes = pl.ds(pl.multiple_of(t * 128, 128), 128)
            for b in range(4):
                rows = slice(b * 128, (b + 1) * 128)
                scores = (xt[rows, lanes] + acol[rows, :]).reshape(16, 8, 128)
                peak = jnp.max(scores, axis=0)
                total = jnp.sum(jnp.exp2(scores - peak[None]), axis=0)
                fparts[b * 8 : (b + 1) * 8, lanes] = peak + log2(total)
            return carry

        lax.fori_loop(0, NI // 128, tile, 0)
        out[...] = merge_rows(fparts[...])

    def f_round(it):
        f_local(lf.at[it, 0])
        for dx in X_PEERS:
            send(lf.at[it, 0], lfx.at[it, dx - 1], fx_s.at[it], fx_r.at[it], dx=dx)
        if it == 0:
            for z2 in range(NZ):
                own[z2 * OWN : (z2 + 1) * OWN, :] = src[pl.ds(pl.multiple_of((z2 * NX + x) * OWN, OWN), OWN), :]
        wait(lfx.at[it], fx_r.at[it])
        lf[it, 1] = merge([lf[it, 0]] + [lfx[it, dx - 1] for dx in X_PEERS])
        for dz in Z_PEERS:
            send(lf.at[it, 1], lfz.at[it, dz - 1], fz_s.at[it], fz_r.at[it], dz=dz)

    def f_end(it, sqx):
        wait(lfz.at[it], fz_r.at[it])
        f2 = sqx - merge([lf[it, 1]] + [lfz[it, dz - 1] for dz in Z_PEERS])
        return ls2 + f2 - sqx

    def g_local(out):
        def group(r, carry):
            rows = pl.ds(pl.multiple_of(r * 8, 8), 8)
            tiles = [
                xt[rows, t * 128 : (t + 1) * 128] + browb[:, t * 128 : (t + 1) * 128] for t in range(NI // 128)
            ]
            peak = functools.reduce(jnp.maximum, tiles)
            total = sum(jnp.exp2(tile - peak) for tile in tiles)
            gparts[rows, :] = peak + log2(total)
            return carry

        lax.fori_loop(0, NJ // 8, group, 0)
        out[...] = merge_rows(gparts[...].T)

    f_round(0)
    sqx = jnp.concatenate(
        [squared_norms(src[c * 256 : (c + 1) * 256, :]) for c in range(NI // 256)], axis=1
    ) * NORM
    brow = f_end(0, sqx)
    browb[...] = jnp.broadcast_to(brow, (8, NI))
    g_local(lg.at[0])
    for n, (dy, dk) in enumerate(ROW_PEERS):
        send(lg.at[0], lgr.at[n], gr_s, gr_r, dy=dy, dk=dk)
    wait(lgr, gr_r)
    g2 = sqy - merge([lg[0]] + [lgr[n] for n in range(len(ROW_PEERS))])
    acol[...] = to_column(lt2 + g2 - sqy)

    f_round(1)
    for dx in X_PEERS:
        wait(trecv.at[dx - 1, half], pf_r.at[dx - 1])
        send(trecv.at[dx - 1, half], trecv.at[dx - 1, half], sib_s, sib_r.at[dx - 1], dk=1)
    brow = f_end(1, sqx)
    browb[...] = jnp.broadcast_to(brow, (8, NI))
    g_local(lg.at[1])
    for n, (dy, dk, dx) in enumerate(WIDE_PEERS):
        send(lg.at[1], lgw.at[n], gw_s, gw_r, dy=dy, dk=dk, dx=dx)

    lcol = to_column(lg[1])
    for b in range(4):
        rows = slice(b * 128, (b + 1) * 128)
        weights = jnp.exp2(xt[rows, :] + brow - lcol[rows, :1]).astype(BF16)
        tn[rows, :] = jnp.dot(weights, src[...], preferred_element_type=F32)
    send(tn.at[other], tsib, ts_s, ts_r, dk=1)

    bcol[...] = to_column(brow)
    for dx in X_PEERS:
        wait(trecv.at[dx - 1, other], sib_r.at[dx - 1])
        t4[dx * NJ : (dx + 1) * NJ, :] = trecv[dx - 1].astype(BF16)
    for dx in range(NX):
        block = slice(dx * NJ, (dx + 1) * NJ)
        x2[:, block] = nt_dot(own[...], t4[block, :]) * (2 * NORM)

    wait(auxr, aux_r)
    wait(lgw, gw_r)
    arow = []
    for b in range(NX):
        parts = [lgw[n] for n, (dy, dk, dx) in enumerate(WIDE_PEERS) if dx == b]
        if b == 0:
            total = merge([lg[1]] + parts)
            arow.append(lt2 + (sqy - total) - sqy)
            shares = [jnp.exp2(lg[1] - total), jnp.exp2(lgw[WIDE_PEERS.index((0, 1, 0))] - total)]
        else:
            mass, norm = auxr[b - 1, 0:1, :], auxr[b - 1, 1:2, :]
            arow.append(mass + (norm - merge(parts)) - norm)
    arow = jnp.concatenate(arow, axis=1)

    wait(tsib, ts_r)
    dn[0] = shares[0]
    dn[1] = shares[1]
    mine, theirs = to_column(dn[0]), to_column(dn[1])
    gparts[...] = mine
    acol[...] = theirs
    tc[...] = tn[half, :] * gparts[half, :1] + tsib[...] * acol[half, :1]
    for dy in Y_PEERS:
        quarter = pl.ds(pl.multiple_of(lax.rem(y + dy, NY) * QUART, QUART), QUART)
        send(tc.at[quarter], ty.at[dy - 1], ty_s, ty_r, dy=dy)

    for z2 in range(NZ):
        rows = slice(z2 * OWN, (z2 + 1) * OWN)
        bias = bcol[pl.ds(pl.multiple_of((z2 * NX + x) * OWN, OWN), OWN), :1]
        plan = jnp.exp2(x2[rows, :] + bias + arow)
        dparts[rows, :] = sum(plan[:, t * 128 : (t + 1) * 128] for t in range(NX * NJ // 128))
        num[z2] = jnp.dot(plan.astype(BF16), t4[...], preferred_element_type=F32)
    dn[2] = jnp.sum(dparts[...].T, axis=0, keepdims=True)

    def block(dz):
        return num.at[lax.rem(z + dz, NZ)]

    def hop(s, c):
        rows = pl.ds(c * 32, 32)
        if s == 0:
            if c == 0:
                send(block(4).at[pl.ds(0, 32)], plus.at[0, 0], plus_s.at[0, 0], plus_r.at[0, 0], dz=1)
            else:
                send(block(4).at[pl.ds(32, 32)], minus.at[0, 1], minus_s.at[0, 1], minus_r.at[0, 1], dz=NZ - 1)
            return
        for way, buf, ssem, rsem, to in (
            (1, plus, plus_s, plus_r, 1),
            (-1, minus, minus_s, minus_r, NZ - 1),
        ):
            mine = block((way * (4 - s)) % NZ).at[rows]
            if s > 1 or (way == 1) == (c == 0):
                wait(buf.at[s - 1, c], rsem.at[s - 1, c])
                mine[...] = mine[...] + buf[s - 1, c]
            send(mine, buf.at[s, c], ssem.at[s, c], rsem.at[s, c], dz=to)

    hop(0, 0)
    hop(0, 1)
    for dz in Z_PEERS:
        send(dn.at[2], dnr.at[dz - 1], dn_s, dn_r, dz=dz)
    hop(1, 0)
    hop(1, 1)
    hop(2, 0)
    hop(2, 1)

    place = pl.ds(pl.multiple_of(k * HALF + y * QUART, QUART), QUART)
    wait(ty, ty_r)
    tout[place, :] = tc[pl.ds(pl.multiple_of(y * QUART, QUART), QUART), :] + ty[0] + ty[1] + ty[2]
    for dy in Y_PEERS:
        send(tout.at[place], tout.at[place], ta_s, ta_r.at[dy - 1], dy=dy)
    send(tout.at[place], tout.at[place], tb_s, tb_r, dk=1)

    hop(3, 0)
    hop(3, 1)
    for dy in (1, 3, 2):
        theirs = pl.ds(pl.multiple_of(k * HALF + lax.rem(y + NY - dy, NY) * QUART, QUART), QUART)
        wait(tout.at[theirs], ta_r.at[dy - 1])
        send(tout.at[theirs], tout.at[theirs], tb_s, tb_r, dk=1)

    wait(dnr, dn_r)
    denom = dn[2]
    for dz in Z_PEERS:
        denom = denom + dnr[dz - 1]
    dparts[...] = to_column(denom)
    inverse = 1.0 / dparts[pl.ds(pl.multiple_of(z * OWN, OWN), OWN), :1]
    for c in range(2):
        rows = slice(c * 32, (c + 1) * 32)
        wait(plus.at[3, c], plus_r.at[3, c])
        wait(minus.at[3, c], minus_r.at[3, c])
        simg[rows, :] = (num[z, rows, :] + plus[3, c] + minus[3, c]) * inverse[rows]
    wait(tout.at[other], tb_r)
    timg[...] = tout[...]

    wait(auxr, aux_s)
    wait(trecv.at[:, half], pf_s)
    wait(trecv.at[:, half], sib_s)
    for it in range(2):
        wait(lfx.at[it], fx_s.at[it])
        wait(lfz.at[it], fz_s.at[it])
    wait(lgr, gr_s)
    wait(lgw, gw_s)
    wait(tsib, ts_s)
    wait(ty, ty_s)
    wait(ty, ta_s)
    wait(tout.at[half], tb_s)
    wait(dnr, dn_s)
    for s in range(4):
        for c in range(2):
            if s > 0 or c == 0:
                wait(plus.at[s, c], plus_s.at[s, c])
            if s > 0 or c == 1:
                wait(minus.at[s, c], minus_s.at[s, c])


def on_device(source, target, log_source_mass, log_target_mass):
    dma, vmem = pltpu.SemaphoreType.DMA, pltpu.VMEM
    scratch = [
        vmem((NJ, NI), F32),
        vmem((NX * OWN * NZ // 4, NX * NJ), F32),
        vmem((NX * NJ, D), BF16),
        vmem((NJ, D), F32),
        vmem((NX - 1, NJ, D), F32),
        vmem((NZ * OWN, D), BF16),
        vmem((32, NI), F32),
        vmem((NJ, 128), F32),
        vmem((NJ, 128), F32),
        vmem((8, NI), F32),
        vmem((NZ, OWN, D), F32),
        vmem((NZ * OWN, 128), F32),
        vmem((2, NJ), F32),
        vmem((NX - 1, 2, NJ), F32),
        vmem((2, 2, 1, NI), F32),
        vmem((2, NX - 1, 1, NI), F32),
        vmem((2, NZ - 1, 1, NI), F32),
        vmem((2, 1, NJ), F32),
        vmem((len(ROW_PEERS), 1, NJ), F32),
        vmem((len(WIDE_PEERS), 1, NJ), F32),
        vmem((NI, 128), F32),
        vmem((NJ, D), F32),
        vmem((HALF, D), F32),
        vmem((HALF, D), F32),
        vmem((NY - 1, QUART, D), F32),
        vmem((NJ, D), F32),
        vmem((4, 2, 32, D), F32),
        vmem((4, 2, 32, D), F32),
        vmem((3, 1, NJ), F32),
        vmem((NZ - 1, 1, NJ), F32),
        dma, dma((3,)), dma, dma((3,)), dma, dma,
        dma((2,)), dma((2,)), dma((2,)), dma((2,)),
        dma, dma, dma, dma,
        dma, dma, dma, dma, dma, dma((3,)), dma, dma,
        dma((4, 2)), dma((4, 2)), dma((4, 2)), dma((4, 2)), dma, dma,
    ]
    return pl.pallas_call(
        kernel,
        out_shape=(jax.ShapeDtypeStruct((OWN, D), F32), jax.ShapeDtypeStruct((NJ, D), F32)),
        in_specs=[pl.BlockSpec(memory_space=vmem)] * 4,
        out_specs=(pl.BlockSpec(memory_space=vmem),) * 2,
        scratch_shapes=scratch,
        compiler_params=pltpu.CompilerParams(
            collective_id=0, has_side_effects=True, vmem_limit_bytes=56 * 2**20
        ),
        cost_estimate=pl.CostEstimate(flops=8 * NI * NJ * D, bytes_accessed=4 * 2**20, transcendentals=7 * NI * NJ),
        name="sinkhorn",
    )(source, target, log_source_mass.reshape(1, NI), log_target_mass.reshape(1, NJ))


def solution(mesh):
    in_specs = (P("row", None), P("col", None), P("row"), P("col"))
    out_specs = (P(("row", "col"), None), P("col", None))
    return jax.shard_map(
        on_device, mesh=mesh, in_specs=in_specs, out_specs=out_specs, check_vma=False
    )
```

```python
import functools
import math

import jax
import jax.numpy as jnp
from jax import lax
from jax.experimental import pallas as pl
from jax.experimental.pallas import tpu as pltpu
from jax.sharding import PartitionSpec as P

D = 512
NI = 2048
NJ = 512
NY, NK, NZ, NX = 4, 2, 8, 4
OWN = NI // (NZ * NX)
HALF = NJ // NK
QUART = HALF // NY
BLUR = 0.1
LOG2E = math.log2(math.e)
NORM = LOG2E / (D * BLUR)
MESH = pl.DeviceIdType.MESH
F32 = jnp.float32
BF16 = jnp.bfloat16

X_PEERS = [1, 2, 3]
Y_PEERS = [2, 1, 3]
Z_PEERS = [4, 3, 5, 2, 6, 1, 7]
ROW_PEERS = [(dy, dk) for dy in (2, 1, 3, 0) for dk in (1, 0) if (dy, dk) != (0, 0)]
WIDE_PEERS = [
    (dy, dk, dx) for dy in (2, 1, 3, 0) for dx in (2, 1, 3, 0) for dk in (1, 0) if (dy, dk, dx) != (0, 0, 0)
]


BARRIER_PEERS = (
    [(0, 0, dz, 0) for dz in Z_PEERS] + [(dy, dk, 0, 0) for dy, dk in ROW_PEERS] + [(0, 0, 0, dx) for dx in X_PEERS]
)


def log2(x):
    return jnp.log(x) * LOG2E


def merge(parts):
    peak = functools.reduce(jnp.maximum, parts)
    return peak + log2(sum(jnp.exp2(part - peak) for part in parts))


def merge_rows(x):
    peak = jnp.max(x, axis=0, keepdims=True)
    return peak + log2(jnp.sum(jnp.exp2(x - peak), axis=0, keepdims=True))


def to_column(row):
    return jnp.broadcast_to(row, (128, row.shape[1])).T


def nt_dot(a, b):
    return lax.dot_general(a, b, (((1,), (1,)), ((), ())), preferred_element_type=F32)


def squared_norms(x):
    sq = x.astype(F32)
    sq = sq * sq
    high = sq.astype(BF16)
    low = (sq - high.astype(F32)).astype(BF16)
    ones = jnp.ones((8, D), BF16)
    return (nt_dot(ones, high) + nt_dot(ones, low))[:1]


def kernel(
    src_in, tgt_in, lsm_in, ltm_in, simg, timg,
    src, tgt, lsm, ltm, in_sem,
    xt, x2, t4, tf, trecv, own, fparts, gparts, acol, browb, num, dparts, arowb, brown, weights,
    aux, auxr, lf, lfx, lfz, lg, lgr, lgw, bcol,
    tn, tsib, tc, ty, tout, plus, minus, dn, dnr,
    pf_s, pf_r, pfn_s, pfn_r, pff_s, pff_r, gw1_s, gw1_r, sib_s, sib_r, aux_s, aux_r, fx_s, fx_r, fz_s, fz_r, gr_s, gr_r, gw_s, gw_r,
    ts_s, ts_r, ty_s, ty_r, ta_s, ta_r, tb_s, tb_r, plus_s, plus_r, minus_s, minus_r, dn_s, dn_r,
):
    row, col = lax.axis_index("row"), lax.axis_index("col")
    y, k, z, x = row // NK, row % NK, col // NX, col % NX

    def dev(dy=0, dk=0, dz=0, dx=0):
        return {
            "row": lax.rem(y + dy, NY) * NK + lax.rem(k + dk, NK),
            "col": lax.rem(z + dz, NZ) * NX + lax.rem(x + dx, NX),
        }

    def send(source, target, send_sem, recv_sem, **to):
        copy = pltpu.make_async_remote_copy(
            source, target, send_sem, recv_sem, device_id=dev(**to), device_id_type=MESH
        )
        copy.start()

    def wait(ref, sem):
        pltpu.make_async_copy(ref, ref, sem).wait()

    barrier = pltpu.get_barrier_semaphore()
    for peer in BARRIER_PEERS:
        pl.semaphore_signal(barrier, 1, device_id=dev(*peer), device_id_type=MESH)
    loads = [
        pltpu.make_async_copy(ref, held, in_sem.at[n])
        for n, (ref, held) in enumerate(((tgt_in, tgt), (src_in, src), (ltm_in, ltm), (lsm_in, lsm)))
    ]
    for load in loads:
        load.start()
    for load in loads:
        load.wait()

    ls2 = lsm[...] * LOG2E
    lt2 = ltm[...] * LOG2E
    sqy = squared_norms(tgt[...]) * NORM
    aux[0:1, :] = lt2
    aux[1:2, :] = sqy
    acol[...] = to_column(lt2 - sqy)
    half = pl.ds(pl.multiple_of(k * HALF, HALF), HALF)
    other = pl.ds(pl.multiple_of((1 - k) * HALF, HALF), HALF)
    near = pl.ds(pl.multiple_of(k * HALF, HALF), HALF // 2)
    far = pl.ds(pl.multiple_of(k * HALF + HALF // 2, HALF // 2), HALF // 2)
    for c in range(NI // 256):
        xt[:, c * 256 : (c + 1) * 256] = nt_dot(tgt[...], src[c * 256 : (c + 1) * 256, :]) * (2 * NORM)

    def f_local(out):
        def tile(t, carry):
            lanes = pl.ds(pl.multiple_of(t * 128, 128), 128)
            for b in range(4):
                rows = slice(b * 128, (b + 1) * 128)
                scores = (xt[rows, lanes] + acol[rows, :]).reshape(16, 8, 128)
                peak = jnp.max(scores, axis=0)
                total = jnp.sum(jnp.exp2(scores - peak[None]), axis=0)
                fparts[b * 8 : (b + 1) * 8, lanes] = peak + log2(total)
            return carry

        lax.fori_loop(0, NI // 128, tile, 0, unroll=8)
        out[...] = merge_rows(fparts[...])

    def f_round(it):
        for dx in X_PEERS:
            send(lf.at[it, 0], lfx.at[it, dx - 1], fx_s.at[it], fx_r.at[it], dx=dx)
        wait(lfx.at[it], fx_r.at[it])
        lf[it, 1] = merge([lf[it, 0]] + [lfx[it, dx - 1] for dx in X_PEERS])
        for dz in Z_PEERS:
            send(lf.at[it, 1], lfz.at[it, dz - 1], fz_s.at[it], fz_r.at[it], dz=dz)

    def f_end(it, sqx):
        wait(lfz.at[it], fz_r.at[it])
        f2 = sqx - merge([lf[it, 1]] + [lfz[it, dz - 1] for dz in Z_PEERS])
        return ls2 + f2 - sqx

    def g_local(out):
        def group(r, carry):
            rows = pl.ds(pl.multiple_of(r * 8, 8), 8)
            tiles = [
                xt[rows, t * 128 : (t + 1) * 128] + browb[:, t * 128 : (t + 1) * 128] for t in range(NI // 128)
            ]
            peak = functools.reduce(jnp.maximum, tiles)
            total = sum(jnp.exp2(tile - peak) for tile in tiles)
            gparts[rows, :] = peak + log2(total)
            return carry

        lax.fori_loop(0, NJ // 8, group, 0, unroll=16)
        out[...] = merge_rows(gparts[...].T)

    f_local(lf.at[0, 0])
    tf[...] = tgt[...].astype(F32)
    t4[:NJ, :] = tgt[...]
    for z2 in range(NZ):
        own[z2 * OWN : (z2 + 1) * OWN, :] = src[pl.ds(pl.multiple_of((z2 * NX + x) * OWN, OWN), OWN), :]
    pl.semaphore_wait(barrier, len(BARRIER_PEERS))
    f_round(0)
    for dx in X_PEERS:
        send(aux, auxr.at[dx - 1], aux_s, aux_r, dx=dx)
    for dx in (1, 3):
        send(tf.at[half], trecv.at[dx - 1, half], pf_s.at[dx - 1], pf_r.at[dx - 1], dx=dx)
    sqx = jnp.concatenate(
        [squared_norms(src[c * 256 : (c + 1) * 256, :]) for c in range(NI // 256)], axis=1
    ) * NORM
    brow = f_end(0, sqx)
    browb[...] = jnp.broadcast_to(brow, (8, NI))
    g_local(lg.at[0])
    for n, (dy, dk) in enumerate(ROW_PEERS):
        send(lg.at[0], lgr.at[n], gr_s, gr_r, dy=dy, dk=dk)
    wait(lgr, gr_r)
    g2 = sqy - merge([lg[0]] + [lgr[n] for n in range(len(ROW_PEERS))])
    acol[...] = to_column(lt2 + g2 - sqy)

    f_local(lf.at[1, 0])
    f_round(1)
    for dx in (1, 3):
        wait(trecv.at[dx - 1, half], pf_r.at[dx - 1])
    send(trecv.at[0, near], trecv.at[1, near], pfn_s, pfn_r, dx=1)
    send(trecv.at[2, far], trecv.at[1, far], pff_s, pff_r, dx=3)
    for dx in (1, 3):
        send(trecv.at[dx - 1, half], trecv.at[dx - 1, half], sib_s.at[dx - 1], sib_r.at[dx - 1], dk=1)
    brow = f_end(1, sqx)
    browb[...] = jnp.broadcast_to(brow, (8, NI))
    g_local(lg.at[1])
    for n, (dy, dk, dx) in enumerate(WIDE_PEERS):
        if (dy, dk, dx) == (0, 1, 0):
            send(lg.at[1], lgw.at[n], gw1_s, gw1_r, dy=dy, dk=dk, dx=dx)
        else:
            send(lg.at[1], lgw.at[n], gw_s, gw_r, dy=dy, dk=dk, dx=dx)

    lcol = to_column(lg[1])
    for b in range(4):
        rows = slice(b * 128, (b + 1) * 128)
        shares = jnp.exp2(xt[rows, :] + brow - lcol[rows, :1]).astype(BF16)
        tn[rows, :] = jnp.dot(shares, src[...], preferred_element_type=F32)
    send(tn.at[other], tsib, ts_s, ts_r, dk=1)

    def wide_scores(dx):
        block = slice(dx * NJ, (dx + 1) * NJ)
        if dx > 0:
            wait(trecv.at[dx - 1, other], sib_r.at[dx - 1])
            t4[block, :] = trecv[dx - 1].astype(BF16)
        x2[:, block] = nt_dot(own[...], t4[block, :]) * (2 * NORM)

    wait(trecv.at[1, near], pfn_r)
    wait(trecv.at[1, far], pff_r)
    send(trecv.at[1, half], trecv.at[1, half], sib_s.at[1], sib_r.at[1], dk=1)
    bcol[...] = to_column(brow)
    wide_scores(0)
    wide_scores(1)
    wide_scores(3)

    wait(lgw.at[0], gw1_r)
    sibling = WIDE_PEERS.index((0, 1, 0))
    pair = merge([lg[1], lgw[sibling]])
    gparts[...] = to_column(jnp.exp2(lg[1] - pair))
    acol[...] = to_column(jnp.exp2(lgw[sibling] - pair))
    wait(tsib, ts_r)
    tc[...] = tn[half, :] * gparts[half, :1] + tsib[...] * acol[half, :1]
    for dy in Y_PEERS:
        quarter = pl.ds(pl.multiple_of(lax.rem(y + dy, NY) * QUART, QUART), QUART)
        send(tc.at[quarter], ty.at[dy - 1], ty_s, ty_r, dy=dy)
    wide_scores(2)

    wait(auxr, aux_r)
    wait(lgw.at[pl.ds(0, len(WIDE_PEERS) - 1)], gw_r)
    arow = []
    for b in range(NX):
        parts = {dk + NK * dy: lgw[n] for n, (dy, dk, dx) in enumerate(WIDE_PEERS) if dx == b}
        if b == 0:
            parts[0] = lg[1]
            total = merge(list(parts.values()))
            arow.append(lt2 + (sqy - total) - sqy)
            for dy in range(NY):
                dn[dy] = jnp.exp2(merge([parts[NK * dy], parts[NK * dy + 1]]) - total)
        else:
            mass, norm = auxr[b - 1, 0:1, :], auxr[b - 1, 1:2, :]
            arow.append(mass + (norm - merge(list(parts.values()))) - norm)
    arowb[...] = jnp.broadcast_to(jnp.concatenate(arow, axis=1), (16, NX * NJ))

    for z2 in range(NZ):
        rows = slice(z2 * OWN, (z2 + 1) * OWN)
        brown[rows, :] = bcol[pl.ds(pl.multiple_of((z2 * NX + x) * OWN, OWN), OWN), :]

    def plan_rows(r, carry):
        rows = pl.ds(pl.multiple_of(r * 16, 16), 16)
        bias = brown[rows, :]
        denom = None
        for t in range(NX * NJ // 128):
            lanes = slice(t * 128, (t + 1) * 128)
            plan = jnp.exp2(x2[rows, lanes] + bias + arowb[:, lanes])
            denom = plan if denom is None else denom + plan
            weights[rows, lanes] = plan.astype(BF16)
        dparts[rows, :] = denom
        return carry

    lax.fori_loop(0, NZ * OWN // 16, plan_rows, 0, unroll=4)
    for b in range(4):
        sums = jnp.dot(weights[b * 128 : (b + 1) * 128, :], t4[...], preferred_element_type=F32)
        num[2 * b] = sums[:OWN]
        num[2 * b + 1] = sums[OWN:]

    def block(dz):
        return num.at[lax.rem(z + dz, NZ)]

    def hop(s, c):
        rows = pl.ds(c * 32, 32)
        if s == 0:
            if c == 0:
                send(block(4).at[pl.ds(0, 32)], plus.at[0, 0], plus_s.at[0, 0], plus_r.at[0, 0], dz=1)
            else:
                send(block(4).at[pl.ds(32, 32)], minus.at[0, 1], minus_s.at[0, 1], minus_r.at[0, 1], dz=NZ - 1)
            return
        for way, buf, ssem, rsem, to in (
            (1, plus, plus_s, plus_r, 1),
            (-1, minus, minus_s, minus_r, NZ - 1),
        ):
            mine = block((way * (4 - s)) % NZ).at[rows]
            if s > 1 or (way == 1) == (c == 0):
                wait(buf.at[s - 1, c], rsem.at[s - 1, c])
                mine[...] = mine[...] + buf[s - 1, c]
            send(mine, buf.at[s, c], ssem.at[s, c], rsem.at[s, c], dz=to)

    hop(0, 0)
    hop(0, 1)
    dn[NY] = jnp.sum(dparts[...].T, axis=0, keepdims=True)
    for dz in Z_PEERS:
        send(dn.at[NY], dnr.at[dz - 1], dn_s, dn_r, dz=dz)

    place = pl.ds(pl.multiple_of(k * HALF + y * QUART, QUART), QUART)
    rows = pl.ds(pl.multiple_of(y * QUART, QUART), QUART)
    wait(ty, ty_r)
    for dy in range(NY):
        gparts[...] = to_column(dn[dy])
        part = (tc[rows, :] if dy == 0 else ty[dy - 1]) * gparts[place, :1]
        whole = part if dy == 0 else whole + part
    tout[place, :] = whole
    for dy in Y_PEERS:
        send(tout.at[place], tout.at[place], ta_s, ta_r.at[dy - 1], dy=dy)
    send(tout.at[place], tout.at[place], tb_s, tb_r, dk=1)

    hop(1, 0)
    hop(1, 1)
    hop(2, 0)
    hop(2, 1)
    hop(3, 0)
    hop(3, 1)
    for dy in (1, 3, 2):
        theirs = pl.ds(pl.multiple_of(k * HALF + lax.rem(y + NY - dy, NY) * QUART, QUART), QUART)
        wait(tout.at[theirs], ta_r.at[dy - 1])
        send(tout.at[theirs], tout.at[theirs], tb_s, tb_r, dk=1)

    wait(dnr, dn_r)
    denom = dn[NY]
    for dz in Z_PEERS:
        denom = denom + dnr[dz - 1]
    dparts[...] = to_column(denom)
    inverse = 1.0 / dparts[pl.ds(pl.multiple_of(z * OWN, OWN), OWN), :1]
    for c in range(2):
        rows = slice(c * 32, (c + 1) * 32)
        wait(plus.at[3, c], plus_r.at[3, c])
        wait(minus.at[3, c], minus_r.at[3, c])
        simg[rows, :] = (num[z, rows, :] + plus[3, c] + minus[3, c]) * inverse[rows]
    wait(tout.at[other], tb_r)
    timg[...] = tout[...]

    wait(auxr, aux_s)
    for dx in (1, 3):
        wait(trecv.at[dx - 1, half], pf_s.at[dx - 1])
    wait(trecv.at[1, near], pfn_s)
    wait(trecv.at[1, far], pff_s)
    for dx in X_PEERS:
        wait(trecv.at[dx - 1, half], sib_s.at[dx - 1])
    for it in range(2):
        wait(lfx.at[it], fx_s.at[it])
        wait(lfz.at[it], fz_s.at[it])
    wait(lgr, gr_s)
    wait(lgw.at[0], gw1_s)
    wait(lgw.at[pl.ds(0, len(WIDE_PEERS) - 1)], gw_s)
    wait(tsib, ts_s)
    wait(ty, ty_s)
    wait(ty, ta_s)
    wait(tout.at[half], tb_s)
    wait(dnr, dn_s)
    for s in range(4):
        for c in range(2):
            if s > 0 or c == 0:
                wait(plus.at[s, c], plus_s.at[s, c])
            if s > 0 or c == 1:
                wait(minus.at[s, c], minus_s.at[s, c])


def hand_over(simg, timg, simg_out, timg_out):
    simg_out[...] = simg[...]
    timg_out[...] = timg[...]


def on_device(source, target, log_source_mass, log_target_mass):
    dma, vmem = pltpu.SemaphoreType.DMA, pltpu.VMEM
    scratch = [
        vmem((NI, D), BF16),
        vmem((NJ, D), BF16),
        vmem((1, NI), F32),
        vmem((1, NJ), F32),
        dma((4,)),
        vmem((NJ, NI), F32),
        vmem((NZ * OWN, NX * NJ), F32),
        vmem((NX * NJ, D), BF16),
        vmem((NJ, D), F32),
        vmem((NX - 1, NJ, D), F32),
        vmem((NZ * OWN, D), BF16),
        vmem((32, NI), F32),
        vmem((NJ, 128), F32),
        vmem((NJ, 128), F32),
        vmem((8, NI), F32),
        vmem((NZ, OWN, D), F32),
        vmem((NZ * OWN, 128), F32),
        vmem((16, NX * NJ), F32),
        vmem((NZ * OWN, 128), F32),
        vmem((NZ * OWN, NX * NJ), BF16),
        vmem((2, NJ), F32),
        vmem((NX - 1, 2, NJ), F32),
        vmem((2, 2, 1, NI), F32),
        vmem((2, NX - 1, 1, NI), F32),
        vmem((2, NZ - 1, 1, NI), F32),
        vmem((2, 1, NJ), F32),
        vmem((len(ROW_PEERS), 1, NJ), F32),
        vmem((len(WIDE_PEERS), 1, NJ), F32),
        vmem((NI, 128), F32),
        vmem((NJ, D), F32),
        vmem((HALF, D), F32),
        vmem((HALF, D), F32),
        vmem((NY - 1, QUART, D), F32),
        vmem((NJ, D), F32),
        vmem((4, 2, 32, D), F32),
        vmem((4, 2, 32, D), F32),
        vmem((NY + 1, 1, NJ), F32),
        vmem((NZ - 1, 1, NJ), F32),
        dma((3,)), dma((3,)), dma, dma, dma, dma, dma, dma,
        dma((3,)), dma((3,)), dma, dma,
        dma((2,)), dma((2,)), dma((2,)), dma((2,)),
        dma, dma, dma, dma,
        dma, dma, dma, dma, dma, dma((3,)), dma, dma,
        dma((4, 2)), dma((4, 2)), dma((4, 2)), dma((4, 2)), dma, dma,
    ]
    images = pl.pallas_call(
        kernel,
        out_shape=(jax.ShapeDtypeStruct((OWN, D), F32), jax.ShapeDtypeStruct((NJ, D), F32)),
        in_specs=[pl.BlockSpec(memory_space=pl.ANY)] * 4,
        out_specs=(pl.BlockSpec(memory_space=vmem),) * 2,
        scratch_shapes=scratch,
        compiler_params=pltpu.CompilerParams(
            collective_id=0, has_side_effects=True, vmem_limit_bytes=56 * 2**20
        ),
        cost_estimate=pl.CostEstimate(flops=8 * NI * NJ * D, bytes_accessed=4 * 2**20, transcendentals=7 * NI * NJ),
        name="sinkhorn",
    )(source, target, log_source_mass.reshape(1, NI), log_target_mass.reshape(1, NJ))
    return pl.pallas_call(
        hand_over,
        out_shape=(jax.ShapeDtypeStruct((OWN, D), F32), jax.ShapeDtypeStruct((NJ, D), F32)),
        in_specs=[pl.BlockSpec(memory_space=vmem)] * 2,
        out_specs=(pl.BlockSpec(memory_space=vmem),) * 2,
        name="hand_over",
    )(*images)


def solution(mesh):
    in_specs = (P("row", None), P("col", None), P("row"), P("col"))
    out_specs = (P(("row", "col"), None), P("col", None))
    return jax.shard_map(
        on_device, mesh=mesh, in_specs=in_specs, out_specs=out_specs, check_vma=False
    )
```

```python
import functools
import math

import jax
import jax.numpy as jnp
from jax import lax
from jax.experimental import pallas as pl
from jax.experimental.pallas import tpu as pltpu
from jax.sharding import PartitionSpec as P

D = 512
NI = 2048
NJ = 512
NY, NK, NZ, NX = 4, 2, 8, 4
OWN = NI // (NZ * NX)
HALF = NJ // NK
QUART = HALF // NY
BLUR = 0.1
LOG2E = math.log2(math.e)
NORM = LOG2E / (D * BLUR)
MESH = pl.DeviceIdType.MESH
F32 = jnp.float32
BF16 = jnp.bfloat16

STEP = 16
PARTS = OWN // STEP
ORDER = [4, 3, 5, 2, 6, 1, 7, 0]
X_PEERS = [1, 2, 3]
Y_PEERS = [2, 1, 3]
Z_PEERS = [4, 3, 5, 2, 6, 1, 7]
ROW_PEERS = [(dy, dk) for dy in (2, 1, 3, 0) for dk in (1, 0) if (dy, dk) != (0, 0)]
WIDE_PEERS = [
    (dy, dk, dx) for dy in (2, 1, 3, 0) for dx in (2, 1, 3, 0) for dk in (1, 0) if (dy, dk, dx) != (0, 0, 0)
]


BARRIER_PEERS = (
    [(0, 0, dz, 0) for dz in Z_PEERS] + [(dy, dk, 0, 0) for dy, dk in ROW_PEERS] + [(0, 0, 0, dx) for dx in X_PEERS]
)


def log2(x):
    return jnp.log(x) * LOG2E


def merge(parts):
    peak = functools.reduce(jnp.maximum, parts)
    return peak + log2(sum(jnp.exp2(part - peak) for part in parts))


def merge_rows(x):
    peak = jnp.max(x, axis=0, keepdims=True)
    return peak + log2(jnp.sum(jnp.exp2(x - peak), axis=0, keepdims=True))


def to_column(row):
    return jnp.broadcast_to(row, (128, row.shape[1])).T


def to_columns(rows):
    rows = rows + [jnp.zeros((128 - len(rows), rows[0].shape[1]), F32)]
    return jnp.concatenate(rows, axis=0).T


def nt_dot(a, b):
    return lax.dot_general(a, b, (((1,), (1,)), ((), ())), preferred_element_type=F32)


def squared_norms(x):
    sq = x.astype(F32)
    sq = sq * sq
    high = sq.astype(BF16)
    low = (sq - high.astype(F32)).astype(BF16)
    ones = jnp.ones((8, D), BF16)
    return (nt_dot(ones, high) + nt_dot(ones, low))[:1]


def kernel(
    src_in, tgt_in, lsm_in, ltm_in, simg_out, timg_out,
    simg, out_sem,    src, tgt, lsm, ltm, in_sem,
    xt, x2, t4, tf, trecv, own, fparts, gparts, acol, browb, num, dparts, arowb, brown, weights,
    aux, auxr, lf, lfx, lfz, lg, lgr, lgw, bcol,
    tn, tsib, tc, ty, tout, plus, minus, dn, dnr,
    pf_s, pf_r, pfn_s, pfn_r, pff_s, pff_r, gw1_s, gw1_r, sib_s, sib_r, aux_s, aux_r, fx_s, fx_r, fz_s, fz_r, gr_s, gr_r, gw_s, gw_r,
    ts_s, ts_r, ty_s, ty_r, ta_s, ta_r, tb_s, tb_r, plus_s, plus_r, minus_s, minus_r, dn_s, dn_r,
):
    row, col = lax.axis_index("row"), lax.axis_index("col")
    y, k, z, x = row // NK, row % NK, col // NX, col % NX

    def dev(dy=0, dk=0, dz=0, dx=0):
        return {
            "row": lax.rem(y + dy, NY) * NK + lax.rem(k + dk, NK),
            "col": lax.rem(z + dz, NZ) * NX + lax.rem(x + dx, NX),
        }

    def send(source, target, send_sem, recv_sem, **to):
        copy = pltpu.make_async_remote_copy(
            source, target, send_sem, recv_sem, device_id=dev(**to), device_id_type=MESH
        )
        copy.start()

    def theirs(dz):
        return pl.ds(pl.multiple_of((lax.rem(z + dz, NZ) * NX + x) * OWN, OWN), OWN)

    def wait(ref, sem):
        pltpu.make_async_copy(ref, ref, sem).wait()

    barrier = pltpu.get_barrier_semaphore()
    for peer in BARRIER_PEERS:
        pl.semaphore_signal(barrier, 1, device_id=dev(*peer), device_id_type=MESH)
    loads = [
        pltpu.make_async_copy(ref, held, in_sem.at[n])
        for n, (ref, held) in enumerate(((tgt_in, tgt), (src_in, src), (ltm_in, ltm), (lsm_in, lsm)))
    ]
    for load in loads:
        load.start()
    for load in loads:
        load.wait()

    ls2 = lsm[...] * LOG2E
    lt2 = ltm[...] * LOG2E
    sqy = squared_norms(tgt[...]) * NORM
    aux[0:1, :] = lt2
    aux[1:2, :] = sqy
    acol[...] = to_column(lt2 - sqy)
    half = pl.ds(pl.multiple_of(k * HALF, HALF), HALF)
    other = pl.ds(pl.multiple_of((1 - k) * HALF, HALF), HALF)
    near = pl.ds(pl.multiple_of(k * HALF, HALF), HALF // 2)
    far = pl.ds(pl.multiple_of(k * HALF + HALF // 2, HALF // 2), HALF // 2)
    for c in range(NI // 256):
        xt[:, c * 256 : (c + 1) * 256] = nt_dot(tgt[...], src[c * 256 : (c + 1) * 256, :]) * (2 * NORM)

    def f_local(out):
        def tile(t, carry):
            lanes = pl.ds(pl.multiple_of(t * 128, 128), 128)
            for b in range(4):
                rows = slice(b * 128, (b + 1) * 128)
                scores = (xt[rows, lanes] + acol[rows, :]).reshape(16, 8, 128)
                peak = jnp.max(scores, axis=0)
                total = jnp.sum(jnp.exp2(scores - peak[None]), axis=0)
                fparts[b * 8 : (b + 1) * 8, lanes] = peak + log2(total)
            return carry

        lax.fori_loop(0, NI // 128, tile, 0, unroll=8)
        out[...] = merge_rows(fparts[...])

    def f_round(it):
        for dx in X_PEERS:
            send(lf.at[it, 0], lfx.at[it, dx - 1], fx_s.at[it], fx_r.at[it], dx=dx)
        wait(lfx.at[it], fx_r.at[it])
        lf[it, 1] = merge([lf[it, 0]] + [lfx[it, dx - 1] for dx in X_PEERS])
        for dz in Z_PEERS:
            send(lf.at[it, 1], lfz.at[it, dz - 1], fz_s.at[it], fz_r.at[it], dz=dz)

    def f_end(it, sqx):
        wait(lfz.at[it], fz_r.at[it])
        f2 = sqx - merge([lf[it, 1]] + [lfz[it, dz - 1] for dz in Z_PEERS])
        return ls2 + f2 - sqx

    def g_local(out):
        def group(r, carry):
            rows = pl.ds(pl.multiple_of(r * 8, 8), 8)
            tiles = [
                xt[rows, t * 128 : (t + 1) * 128] + browb[:, t * 128 : (t + 1) * 128] for t in range(NI // 128)
            ]
            peak = functools.reduce(jnp.maximum, tiles)
            total = sum(jnp.exp2(tile - peak) for tile in tiles)
            gparts[rows, :] = peak + log2(total)
            return carry

        lax.fori_loop(0, NJ // 8, group, 0, unroll=16)
        out[...] = merge_rows(gparts[...].T)

    def wide_scores(dx):
        block = slice(dx * NJ, (dx + 1) * NJ)
        if dx > 0:
            wait(trecv.at[dx - 1, other], sib_r.at[dx - 1])
            t4[block, :] = trecv[dx - 1].astype(BF16)
        x2[:, block] = nt_dot(own[...], t4[block, :]) * (2 * NORM)

    f_local(lf.at[0, 0])
    tf[...] = tgt[...].astype(F32)
    t4[:NJ, :] = tgt[...]
    for n, dz in enumerate(ORDER):
        own[n * OWN : (n + 1) * OWN, :] = src[theirs(dz), :]
    pl.semaphore_wait(barrier, len(BARRIER_PEERS))
    f_round(0)
    for dx in X_PEERS:
        send(aux, auxr.at[dx - 1], aux_s, aux_r, dx=dx)
    for dx in (1, 3):
        send(tf.at[half], trecv.at[dx - 1, half], pf_s.at[dx - 1], pf_r.at[dx - 1], dx=dx)
    sqx = jnp.concatenate(
        [squared_norms(src[c * 256 : (c + 1) * 256, :]) for c in range(NI // 256)], axis=1
    ) * NORM
    brow = f_end(0, sqx)
    browb[...] = jnp.broadcast_to(brow, (8, NI))
    g_local(lg.at[0])
    for n, (dy, dk) in enumerate(ROW_PEERS):
        send(lg.at[0], lgr.at[n], gr_s, gr_r, dy=dy, dk=dk)
    wide_scores(0)
    wait(lgr, gr_r)
    g2 = sqy - merge([lg[0]] + [lgr[n] for n in range(len(ROW_PEERS))])
    acol[...] = to_column(lt2 + g2 - sqy)

    f_local(lf.at[1, 0])
    f_round(1)
    for dx in (1, 3):
        wait(trecv.at[dx - 1, half], pf_r.at[dx - 1])
    send(trecv.at[0, near], trecv.at[1, near], pfn_s, pfn_r, dx=1)
    send(trecv.at[2, far], trecv.at[1, far], pff_s, pff_r, dx=3)
    for dx in (1, 3):
        send(trecv.at[dx - 1, half], trecv.at[dx - 1, half], sib_s.at[dx - 1], sib_r.at[dx - 1], dk=1)
    brow = f_end(1, sqx)
    browb[...] = jnp.broadcast_to(brow, (8, NI))
    g_local(lg.at[1])
    for n, (dy, dk, dx) in enumerate(WIDE_PEERS):
        if (dy, dk, dx) == (0, 1, 0):
            send(lg.at[1], lgw.at[n], gw1_s, gw1_r, dy=dy, dk=dk, dx=dx)
        else:
            send(lg.at[1], lgw.at[n], gw_s, gw_r, dy=dy, dk=dk, dx=dx)

    gparts[...] = to_column(lg[1])
    for b in range(4):
        start = ((1 - k) * HALF if b < 2 else k * HALF) + b % 2 * 128
        rows = pl.ds(pl.multiple_of(start, 128), 128)
        shares = jnp.exp2(xt[rows, :] + brow - gparts[rows, :1]).astype(BF16)
        tn[rows, :] = jnp.dot(shares, src[...], preferred_element_type=F32)
        if b < 2:
            send(tn.at[rows], tsib.at[pl.ds(b * 128, 128)], ts_s.at[b], ts_r.at[b], dk=1)

    wait(trecv.at[1, near], pfn_r)
    wait(trecv.at[1, far], pff_r)
    send(trecv.at[1, half], trecv.at[1, half], sib_s.at[1], sib_r.at[1], dk=1)
    bcol[...] = to_column(brow)
    wide_scores(1)
    wide_scores(3)

    wait(lgw.at[0], gw1_r)
    sibling = WIDE_PEERS.index((0, 1, 0))
    pair = merge([lg[1], lgw[sibling]])
    gparts[...] = to_columns([jnp.exp2(lg[1] - pair), jnp.exp2(lgw[sibling] - pair)])
    for b in range(2):
        wait(tsib.at[pl.ds(b * 128, 128)], ts_r.at[b])
        rows = pl.ds(pl.multiple_of(k * HALF + b * 128, 128), 128)
        part = slice(b * 128, (b + 1) * 128)
        tc[part, :] = tn[rows, :] * gparts[rows, :1] + tsib[part, :] * gparts[rows, 1:2]
    for b in range(2):
        for dy in Y_PEERS:
            start = lax.rem(y + dy, NY) * QUART + b * 32
            send(
                tc.at[pl.ds(pl.multiple_of(start, 32), 32)], ty.at[dy - 1, pl.ds(b * 32, 32)],
                ty_s.at[b], ty_r.at[dy - 1, b], dy=dy,
            )
    wide_scores(2)

    wait(auxr, aux_r)
    wait(lgw.at[pl.ds(0, len(WIDE_PEERS) - 1)], gw_r)
    arow = []
    for b in range(NX):
        parts = {dk + NK * dy: lgw[n] for n, (dy, dk, dx) in enumerate(WIDE_PEERS) if dx == b}
        if b == 0:
            parts[0] = lg[1]
            total = merge(list(parts.values()))
            arow.append(lt2 + (sqy - total) - sqy)
            pairs = [merge([parts[NK * dy], parts[NK * dy + 1]]) for dy in range(NY)]
            gparts[...] = to_columns([jnp.exp2(pair - total) for pair in pairs])
        else:
            mass, norm = auxr[b - 1, 0:1, :], auxr[b - 1, 1:2, :]
            arow.append(mass + (norm - merge(list(parts.values()))) - norm)
    arowb[...] = jnp.broadcast_to(jnp.concatenate(arow, axis=1), (16, NX * NJ))

    for n, dz in enumerate(ORDER):
        brown[n * OWN : (n + 1) * OWN, :] = bcol[theirs(dz), :]

    def plan_rows(r, carry):
        rows = pl.ds(pl.multiple_of(r * 16, 16), 16)
        bias = brown[rows, :]
        denom = None
        for t in range(NX * NJ // 128):
            lanes = slice(t * 128, (t + 1) * 128)
            plan = jnp.exp2(x2[rows, lanes] + bias + arowb[:, lanes])
            denom = plan if denom is None else denom + plan
            weights[rows, lanes] = plan.astype(BF16)
        dparts[rows, :] = denom
        return carry

    def piece(dz, c):
        return num.at[ORDER.index(dz % NZ), pl.ds(c * STEP, STEP)]

    def hop(s, way, c):
        buf, ssem, rsem, to = (plus, plus_s, plus_r, 1) if way == 1 else (minus, minus_s, minus_r, NZ - 1)
        mine = piece(way * (4 - s), c)
        if s > 1 or s == 1 and (way == 1) == (c < PARTS // 2):
            wait(buf.at[s - 1, c], rsem.at[s - 1, c])
            mine[...] = mine[...] + buf[s - 1, c]
        send(mine, buf.at[s, c], ssem.at[s, c], rsem.at[s, c], dz=to)

    low, high = list(range(PARTS // 2)), list(range(PARTS // 2, PARTS))

    def plan_block(b):
        lax.fori_loop(b * 8, (b + 1) * 8, plan_rows, 0, unroll=4)
        sums = jnp.dot(weights[b * 128 : (b + 1) * 128, :], t4[...], preferred_element_type=F32)
        num[2 * b] = sums[:OWN]
        num[2 * b + 1] = sums[OWN:]

    def target_rows(b):
        place = pl.ds(pl.multiple_of(k * HALF + y * QUART + b * 32, 32), 32)
        rows = pl.ds(pl.multiple_of(y * QUART + b * 32, 32), 32)
        shares = gparts[place, :]
        whole = tc[rows, :] * shares[:, :1]
        for dy in Y_PEERS:
            part = ty.at[dy - 1, pl.ds(b * 32, 32)]
            wait(part, ty_r.at[dy - 1, b])
            whole = whole + part[...] * shares[:, dy : dy + 1]
        tout[place, :] = whole
        for dy in Y_PEERS:
            send(tout.at[place], tout.at[place], ta_s, ta_r.at[dy - 1, b], dy=dy)
        send(tout.at[place], tout.at[place], tb_s, tb_r, dk=1)

    def pass_on(dy, b):
        start = k * HALF + lax.rem(y + NY - dy, NY) * QUART + b * 32
        place = pl.ds(pl.multiple_of(start, 32), 32)
        wait(tout.at[place], ta_r.at[dy - 1, b])
        send(tout.at[place], tout.at[place], tb_s, tb_r, dk=1)

    plan_block(0)
    for n in range(PARTS // 2):
        hop(0, 1, low[n])
        hop(0, -1, high[n])
    for c in high:
        hop(1, 1, c)
    plan_block(1)
    for c in low:
        hop(1, -1, c)
    plan_block(2)
    plan_block(3)
    dn[0] = jnp.sum(dparts[...].T, axis=0, keepdims=True)
    for dz in Z_PEERS:
        send(dn.at[0], dnr.at[dz - 1], dn_s, dn_r, dz=dz)
    for n in range(PARTS // 2):
        hop(1, 1, low[n])
        hop(1, -1, high[n])
    target_rows(0)
    for n in range(PARTS // 2):
        hop(2, 1, high[n])
        hop(2, -1, low[n])
    target_rows(1)
    for n in range(PARTS // 2):
        hop(2, 1, low[n])
        hop(2, -1, high[n])
    for n in range(PARTS):
        hop(3, 1, (high + low)[n])
        hop(3, -1, (low + high)[n])
    for b in range(2):
        for dy in (1, 3, 2):
            pass_on(dy, b)
    mine = pltpu.make_async_copy(tout.at[half], timg_out.at[half], out_sem.at[0])
    mine.start()

    wait(dnr, dn_r)
    first = ORDER.index(0) * OWN
    denom = dn[0, :, first : first + OWN]
    for dz in Z_PEERS:
        first = ORDER.index(dz) * OWN
        denom = denom + dnr[dz - 1, :, first : first + OWN]
    inverse = 1.0 / to_column(jnp.concatenate([denom, denom], axis=1))[:OWN]
    for c in high + low:
        rows = slice(c * STEP, (c + 1) * STEP)
        wait(plus.at[3, c], plus_r.at[3, c])
        wait(minus.at[3, c], minus_r.at[3, c])
        whole = num[ORDER.index(0), rows, :] + plus[3, c] + minus[3, c]
        simg[rows, :] = whole * inverse[rows, :1]
    sources = pltpu.make_async_copy(simg, simg_out, out_sem.at[1])
    sources.start()
    wait(tout.at[other], tb_r)
    swapped = pltpu.make_async_copy(tout.at[other], timg_out.at[other], out_sem.at[2])
    swapped.start()

    wait(auxr, aux_s)
    for dx in (1, 3):
        wait(trecv.at[dx - 1, half], pf_s.at[dx - 1])
    wait(trecv.at[1, near], pfn_s)
    wait(trecv.at[1, far], pff_s)
    for dx in X_PEERS:
        wait(trecv.at[dx - 1, half], sib_s.at[dx - 1])
    for it in range(2):
        wait(lfx.at[it], fx_s.at[it])
        wait(lfz.at[it], fz_s.at[it])
    wait(lgr, gr_s)
    wait(lgw.at[0], gw1_s)
    wait(lgw.at[pl.ds(0, len(WIDE_PEERS) - 1)], gw_s)
    for b in range(2):
        wait(tsib.at[pl.ds(b * 128, 128)], ts_s.at[b])
        wait(ty.at[:, pl.ds(b * 32, 32)], ty_s.at[b])
    wait(ty, ta_s)
    wait(tout.at[half], tb_s)
    wait(dnr, dn_s)
    for s in range(4):
        for c in range(PARTS):
            if s > 0 or c in low:
                wait(plus.at[s, c], plus_s.at[s, c])
            if s > 0 or c in high:
                wait(minus.at[s, c], minus_s.at[s, c])
    mine.wait()
    sources.wait()
    swapped.wait()


def hand_over(simg, timg, simg_out, timg_out):
    simg_out[...] = simg[...]
    timg_out[...] = timg[...]


def on_device(source, target, log_source_mass, log_target_mass):
    dma, vmem = pltpu.SemaphoreType.DMA, pltpu.VMEM
    scratch = [
        vmem((OWN, D), F32),
        dma((3,)),
        vmem((NI, D), BF16),
        vmem((NJ, D), BF16),
        vmem((1, NI), F32),
        vmem((1, NJ), F32),
        dma((4,)),
        vmem((NJ, NI), F32),
        vmem((NZ * OWN, NX * NJ), F32),
        vmem((NX * NJ, D), BF16),
        vmem((NJ, D), F32),
        vmem((NX - 1, NJ, D), F32),
        vmem((NZ * OWN, D), BF16),
        vmem((32, NI), F32),
        vmem((NJ, 128), F32),
        vmem((NJ, 128), F32),
        vmem((8, NI), F32),
        vmem((NZ, OWN, D), F32),
        vmem((NZ * OWN, 128), F32),
        vmem((16, NX * NJ), F32),
        vmem((NZ * OWN, 128), F32),
        vmem((NZ * OWN, NX * NJ), BF16),
        vmem((2, NJ), F32),
        vmem((NX - 1, 2, NJ), F32),
        vmem((2, 2, 1, NI), F32),
        vmem((2, NX - 1, 1, NI), F32),
        vmem((2, NZ - 1, 1, NI), F32),
        vmem((2, 1, NJ), F32),
        vmem((len(ROW_PEERS), 1, NJ), F32),
        vmem((len(WIDE_PEERS), 1, NJ), F32),
        vmem((NI, 128), F32),
        vmem((NJ, D), F32),
        vmem((HALF, D), F32),
        vmem((HALF, D), F32),
        vmem((NY - 1, QUART, D), F32),
        vmem((NJ, D), F32),
        vmem((4, PARTS, STEP, D), F32),
        vmem((4, PARTS, STEP, D), F32),
        vmem((1, 1, NJ), F32),
        vmem((NZ - 1, 1, NJ), F32),
        dma((3,)), dma((3,)), dma, dma, dma, dma, dma, dma,
        dma((3,)), dma((3,)), dma, dma,
        dma((2,)), dma((2,)), dma((2,)), dma((2,)),
        dma, dma, dma, dma,
        dma((2,)), dma((2,)), dma((2,)), dma((3, 2)), dma, dma((3, 2)), dma, dma,
        dma((4, PARTS)), dma((4, PARTS)), dma((4, PARTS)), dma((4, PARTS)), dma, dma,
    ]
    images = pl.pallas_call(
        kernel,
        out_shape=(jax.ShapeDtypeStruct((OWN, D), F32), jax.ShapeDtypeStruct((NJ, D), F32)),
        in_specs=[pl.BlockSpec(memory_space=pl.ANY)] * 4,
        out_specs=(pl.BlockSpec(memory_space=pl.ANY),) * 2,
        scratch_shapes=scratch,
        compiler_params=pltpu.CompilerParams(
            collective_id=0, has_side_effects=True, vmem_limit_bytes=56 * 2**20
        ),
        cost_estimate=pl.CostEstimate(flops=8 * NI * NJ * D, bytes_accessed=4 * 2**20, transcendentals=7 * NI * NJ),
        name="sinkhorn",
    )(source, target, log_source_mass.reshape(1, NI), log_target_mass.reshape(1, NJ))
    return pl.pallas_call(
        hand_over,
        out_shape=(jax.ShapeDtypeStruct((OWN, D), F32), jax.ShapeDtypeStruct((NJ, D), F32)),
        in_specs=[pl.BlockSpec(memory_space=vmem)] * 2,
        out_specs=(pl.BlockSpec(memory_space=vmem),) * 2,
        name="hand_over",
    )(*images)


def solution(mesh):
    in_specs = (P("row", None), P("col", None), P("row"), P("col"))
    out_specs = (P(("row", "col"), None), P("col", None))
    return jax.shard_map(
        on_device, mesh=mesh, in_specs=in_specs, out_specs=out_specs, check_vma=False
    )
```

```python
import functools
import math

import jax
import jax.numpy as jnp
from jax import lax
from jax.experimental import pallas as pl
from jax.experimental.pallas import tpu as pltpu
from jax.sharding import PartitionSpec as P

D = 512
NI = 2048
NJ = 512
NY, NK, NZ, NX = 4, 2, 8, 4
OWN = NI // (NZ * NX)
HALF = NJ // NK
QUART = HALF // NY
BLUR = 0.1
LOG2E = math.log2(math.e)
NORM = LOG2E / (D * BLUR)
MESH = pl.DeviceIdType.MESH
F32 = jnp.float32
BF16 = jnp.bfloat16

STEP = 16
PARTS = OWN // STEP
ORDER = [4, 3, 5, 2, 6, 1, 7, 0]
X_PEERS = [1, 2, 3]
Y_PEERS = [2, 1, 3]
Z_PEERS = [4, 3, 5, 2, 6, 1, 7]
ROW_PEERS = [(dy, dk) for dy in (2, 1, 3, 0) for dk in (1, 0) if (dy, dk) != (0, 0)]
WIDE_PEERS = [
    (dy, dk, dx) for dy in (2, 1, 3, 0) for dx in (2, 1, 3, 0) for dk in (1, 0) if (dy, dk, dx) != (0, 0, 0)
]


BARRIER_PEERS = (
    [(0, 0, dz, 0) for dz in Z_PEERS] + [(dy, dk, 0, 0) for dy, dk in ROW_PEERS] + [(0, 0, 0, dx) for dx in X_PEERS]
)


def log2(x):
    return jnp.log(x) * LOG2E


def merge(parts):
    peak = functools.reduce(jnp.maximum, parts)
    return peak + log2(sum(jnp.exp2(part - peak) for part in parts))


def merge_rows(x):
    peak = jnp.max(x, axis=0, keepdims=True)
    return peak + log2(jnp.sum(jnp.exp2(x - peak), axis=0, keepdims=True))


def to_column(row):
    return jnp.broadcast_to(row, (128, row.shape[1])).T


def to_columns(rows):
    rows = rows + [jnp.zeros((128 - len(rows), rows[0].shape[1]), F32)]
    return jnp.concatenate(rows, axis=0).T


def nt_dot(a, b):
    return lax.dot_general(a, b, (((1,), (1,)), ((), ())), preferred_element_type=F32)


def squared_norms(x):
    sq = x.astype(F32)
    sq = sq * sq
    high = sq.astype(BF16)
    low = (sq - high.astype(F32)).astype(BF16)
    ones = jnp.ones((8, D), BF16)
    return (nt_dot(ones, high) + nt_dot(ones, low))[:1]


def kernel(
    src_in, tgt_in, lsm_in, ltm_in, simg_out, timg_out,
    simg, out_sem,    src, tgt, lsm, ltm, in_sem,
    xt, x2, t4, tf, trecv, own, fparts, gparts, acol, browb, num, dparts, arowb, brown, weights,
    aux, auxr, lf, lfx, lfz, lg, lgr, lgw, bcol,
    tn, tsib, tc, ty, tout, plus, minus, dn, dnr,
    pf_s, pf_r, pfn_s, pfn_r, pff_s, pff_r, gw1_s, gw1_r, sib_s, sib_r, aux_s, aux_r, fx_s, fx_r, fz_s, fz_r, gr_s, gr_r, gw_s, gw_r,
    ts_s, ts_r, ty_s, ty_r, ta_s, ta_r, tb_s, tb_r, plus_s, plus_r, minus_s, minus_r, dn_s, dn_r,
):
    row, col = lax.axis_index("row"), lax.axis_index("col")
    y, k, z, x = row // NK, row % NK, col // NX, col % NX

    def dev(dy=0, dk=0, dz=0, dx=0):
        return {
            "row": lax.rem(y + dy, NY) * NK + lax.rem(k + dk, NK),
            "col": lax.rem(z + dz, NZ) * NX + lax.rem(x + dx, NX),
        }

    def send(source, target, send_sem, recv_sem, **to):
        copy = pltpu.make_async_remote_copy(
            source, target, send_sem, recv_sem, device_id=dev(**to), device_id_type=MESH
        )
        copy.start()

    def theirs(dz):
        return pl.ds(pl.multiple_of((lax.rem(z + dz, NZ) * NX + x) * OWN, OWN), OWN)

    def wait(ref, sem):
        pltpu.make_async_copy(ref, ref, sem).wait()

    barrier = pltpu.get_barrier_semaphore()
    for peer in BARRIER_PEERS:
        pl.semaphore_signal(barrier, 1, device_id=dev(*peer), device_id_type=MESH)
    loads = [
        pltpu.make_async_copy(ref, held, in_sem.at[n])
        for n, (ref, held) in enumerate(((tgt_in, tgt), (ltm_in, ltm), (lsm_in, lsm)))
    ] + [
        pltpu.make_async_copy(
            src_in.at[pl.ds(c * 512, 512)], src.at[pl.ds(c * 512, 512)], in_sem.at[3 + c]
        )
        for c in range(4)
    ]
    for load in loads:
        load.start()
    for load in loads[:3]:
        load.wait()

    ls2 = lsm[...] * LOG2E
    lt2 = ltm[...] * LOG2E
    sqy = squared_norms(tgt[...]) * NORM
    aux[0:1, :] = lt2
    aux[1:2, :] = sqy
    acol[...] = to_column(lt2 - sqy)
    half = pl.ds(pl.multiple_of(k * HALF, HALF), HALF)
    other = pl.ds(pl.multiple_of((1 - k) * HALF, HALF), HALF)
    near = pl.ds(pl.multiple_of(k * HALF, HALF), HALF // 2)
    far = pl.ds(pl.multiple_of(k * HALF + HALF // 2, HALF // 2), HALF // 2)
    def f_tile(t):
        lanes = slice(t * 128, (t + 1) * 128)
        for b in range(4):
            rows = slice(b * 128, (b + 1) * 128)
            scores = (xt[rows, lanes] + acol[rows, :]).reshape(16, 8, 128)
            peak = jnp.max(scores, axis=0)
            total = jnp.sum(jnp.exp2(scores - peak[None]), axis=0)
            fparts[b * 8 : (b + 1) * 8, lanes] = peak + log2(total)

    def f_local(out):
        for t in range(NI // 128):
            f_tile(t)
        out[...] = merge_rows(fparts[...])

    def f_round(it):
        for dx in X_PEERS:
            send(lf.at[it, 0], lfx.at[it, dx - 1], fx_s.at[it], fx_r.at[it], dx=dx)
        if it == 0:
            tf[...] = tgt[...].astype(F32)
            t4[:NJ, :] = tgt[...]
            for n, dz in enumerate(ORDER):
                own[n * OWN : (n + 1) * OWN, :] = src[theirs(dz), :]
        wait(lfx.at[it], fx_r.at[it])
        lf[it, 1] = merge([lf[it, 0]] + [lfx[it, dx - 1] for dx in X_PEERS])
        for dz in Z_PEERS:
            send(lf.at[it, 1], lfz.at[it, dz - 1], fz_s.at[it], fz_r.at[it], dz=dz)

    def f_end(it, sqx):
        wait(lfz.at[it], fz_r.at[it])
        f2 = sqx - merge([lf[it, 1]] + [lfz[it, dz - 1] for dz in Z_PEERS])
        return ls2 + f2 - sqx

    def g_local(out):
        def group(r, carry):
            rows = pl.ds(pl.multiple_of(r * 8, 8), 8)
            tiles = [
                xt[rows, t * 128 : (t + 1) * 128] + browb[:, t * 128 : (t + 1) * 128] for t in range(NI // 128)
            ]
            peak = functools.reduce(jnp.maximum, tiles)
            total = sum(jnp.exp2(tile - peak) for tile in tiles)
            gparts[rows, :] = peak + log2(total)
            return carry

        lax.fori_loop(0, NJ // 8, group, 0, unroll=64)
        out[...] = merge_rows(gparts[...].T)

    def wide_scores(dx):
        block = slice(dx * NJ, (dx + 1) * NJ)
        if dx > 0:
            wait(trecv.at[dx - 1, other], sib_r.at[dx - 1])
            t4[block, :] = trecv[dx - 1].astype(BF16)
        x2[:, block] = nt_dot(own[...], t4[block, :]) * (2 * NORM)

    for c in range(NI // 256):
        if c % 2 == 0:
            loads[3 + c // 2].wait()
        xt[:, c * 256 : (c + 1) * 256] = nt_dot(tgt[...], src[c * 256 : (c + 1) * 256, :]) * (2 * NORM)
        if c > 0:
            f_tile(2 * c - 2)
            f_tile(2 * c - 1)
    f_tile(NI // 128 - 2)
    f_tile(NI // 128 - 1)
    lf[0, 0] = merge_rows(fparts[...])
    pl.semaphore_wait(barrier, len(BARRIER_PEERS))
    f_round(0)
    for dx in X_PEERS:
        send(aux, auxr.at[dx - 1], aux_s, aux_r, dx=dx)
    for dx in (1, 3):
        send(tf.at[half], trecv.at[dx - 1, half], pf_s.at[dx - 1], pf_r.at[dx - 1], dx=dx)
    sqx = jnp.concatenate(
        [squared_norms(src[c * 256 : (c + 1) * 256, :]) for c in range(NI // 256)], axis=1
    ) * NORM
    brow = f_end(0, sqx)
    browb[...] = jnp.broadcast_to(brow, (8, NI))
    g_local(lg.at[0])
    for n, (dy, dk) in enumerate(ROW_PEERS):
        send(lg.at[0], lgr.at[n], gr_s, gr_r, dy=dy, dk=dk)
    wide_scores(0)
    wait(lgr, gr_r)
    g2 = sqy - merge([lg[0]] + [lgr[n] for n in range(len(ROW_PEERS))])
    acol[...] = to_column(lt2 + g2 - sqy)

    f_local(lf.at[1, 0])
    f_round(1)
    for dx in (1, 3):
        wait(trecv.at[dx - 1, half], pf_r.at[dx - 1])
    send(trecv.at[0, near], trecv.at[1, near], pfn_s, pfn_r, dx=1)
    send(trecv.at[2, far], trecv.at[1, far], pff_s, pff_r, dx=3)
    for dx in (1, 3):
        send(trecv.at[dx - 1, half], trecv.at[dx - 1, half], sib_s.at[dx - 1], sib_r.at[dx - 1], dk=1)
    brow = f_end(1, sqx)
    browb[...] = jnp.broadcast_to(brow, (8, NI))
    g_local(lg.at[1])
    for n, (dy, dk, dx) in enumerate(WIDE_PEERS):
        if (dy, dk, dx) == (0, 1, 0):
            send(lg.at[1], lgw.at[n], gw1_s, gw1_r, dy=dy, dk=dk, dx=dx)
        else:
            send(lg.at[1], lgw.at[n], gw_s, gw_r, dy=dy, dk=dk, dx=dx)

    gparts[...] = to_column(lg[1])
    for b in range(4):
        start = ((1 - k) * HALF if b < 2 else k * HALF) + b % 2 * 128
        rows = pl.ds(pl.multiple_of(start, 128), 128)
        shares = jnp.exp2(xt[rows, :] + brow - gparts[rows, :1]).astype(BF16)
        tn[rows, :] = jnp.dot(shares, src[...], preferred_element_type=F32)
        if b < 2:
            send(tn.at[rows], tsib.at[pl.ds(b * 128, 128)], ts_s.at[b], ts_r.at[b], dk=1)

    wait(trecv.at[1, near], pfn_r)
    wait(trecv.at[1, far], pff_r)
    send(trecv.at[1, half], trecv.at[1, half], sib_s.at[1], sib_r.at[1], dk=1)
    wait(lgw.at[0], gw1_r)
    sibling = WIDE_PEERS.index((0, 1, 0))
    pair = merge([lg[1], lgw[sibling]])
    gparts[...] = to_columns([jnp.exp2(lg[1] - pair), jnp.exp2(lgw[sibling] - pair)])
    for b in range(2):
        wait(tsib.at[pl.ds(b * 128, 128)], ts_r.at[b])
        rows = pl.ds(pl.multiple_of(k * HALF + b * 128, 128), 128)
        part = slice(b * 128, (b + 1) * 128)
        tc[part, :] = tn[rows, :] * gparts[rows, :1] + tsib[part, :] * gparts[rows, 1:2]
    for b in range(2):
        for dy in Y_PEERS:
            start = lax.rem(y + dy, NY) * QUART + b * 32
            send(
                tc.at[pl.ds(pl.multiple_of(start, 32), 32)], ty.at[dy - 1, pl.ds(b * 32, 32)],
                ty_s.at[b], ty_r.at[dy - 1, b], dy=dy,
            )
    bcol[...] = to_column(brow)
    for n, dz in enumerate(ORDER):
        brown[n * OWN : (n + 1) * OWN, :] = bcol[theirs(dz), :]
    wide_scores(1)
    wide_scores(3)

    wide_scores(2)

    wait(auxr, aux_r)
    wait(lgw.at[pl.ds(0, len(WIDE_PEERS) - 1)], gw_r)
    arow = []
    for b in range(NX):
        parts = {dk + NK * dy: lgw[n] for n, (dy, dk, dx) in enumerate(WIDE_PEERS) if dx == b}
        if b == 0:
            parts[0] = lg[1]
            total = merge(list(parts.values()))
            arow.append(lt2 + (sqy - total) - sqy)
            pairs = [merge([parts[NK * dy], parts[NK * dy + 1]]) for dy in range(NY)]
            gparts[...] = to_columns([jnp.exp2(pair - total) for pair in pairs])
        else:
            mass, norm = auxr[b - 1, 0:1, :], auxr[b - 1, 1:2, :]
            arow.append(mass + (norm - merge(list(parts.values()))) - norm)
    arowb[...] = jnp.broadcast_to(jnp.concatenate(arow, axis=1), (16, NX * NJ))

    def plan_rows(r, carry):
        rows = pl.ds(pl.multiple_of(r * 16, 16), 16)
        bias = brown[rows, :]
        denom = None
        for t in range(NX * NJ // 128):
            lanes = slice(t * 128, (t + 1) * 128)
            plan = jnp.exp2(x2[rows, lanes] + bias + arowb[:, lanes])
            denom = plan if denom is None else denom + plan
            weights[rows, lanes] = plan.astype(BF16)
        dparts[rows, :] = denom
        return carry

    def piece(dz, c):
        return num.at[ORDER.index(dz % NZ), pl.ds(c * STEP, STEP)]

    def hop(s, way, c):
        buf, ssem, rsem, to = (plus, plus_s, plus_r, 1) if way == 1 else (minus, minus_s, minus_r, NZ - 1)
        mine = piece(way * (4 - s), c)
        if s > 1 or s == 1 and (way == 1) == (c < PARTS // 2):
            wait(buf.at[s - 1, c], rsem.at[s - 1, c])
            mine[...] = mine[...] + buf[s - 1, c]
        send(mine, buf.at[s, c], ssem.at[s, c], rsem.at[s, c], dz=to)

    low, high = list(range(PARTS // 2)), list(range(PARTS // 2, PARTS))

    def plan_block(b):
        lax.fori_loop(b * 8, (b + 1) * 8, plan_rows, 0, unroll=4)
        sums = jnp.dot(weights[b * 128 : (b + 1) * 128, :], t4[...], preferred_element_type=F32)
        num[2 * b] = sums[:OWN]
        num[2 * b + 1] = sums[OWN:]

    def target_rows(b):
        place = pl.ds(pl.multiple_of(k * HALF + y * QUART + b * 32, 32), 32)
        rows = pl.ds(pl.multiple_of(y * QUART + b * 32, 32), 32)
        shares = gparts[place, :]
        whole = tc[rows, :] * shares[:, :1]
        for dy in Y_PEERS:
            part = ty.at[dy - 1, pl.ds(b * 32, 32)]
            wait(part, ty_r.at[dy - 1, b])
            whole = whole + part[...] * shares[:, dy : dy + 1]
        tout[place, :] = whole
        for dy in Y_PEERS:
            send(tout.at[place], tout.at[place], ta_s, ta_r.at[dy - 1, b], dy=dy)
        send(tout.at[place], tout.at[place], tb_s, tb_r, dk=1)

    def pass_on(dy, b):
        start = k * HALF + lax.rem(y + NY - dy, NY) * QUART + b * 32
        place = pl.ds(pl.multiple_of(start, 32), 32)
        wait(tout.at[place], ta_r.at[dy - 1, b])
        send(tout.at[place], tout.at[place], tb_s, tb_r, dk=1)

    plan_block(0)
    for n in range(PARTS // 2):
        hop(0, 1, low[n])
        hop(0, -1, high[n])
    for c in high:
        hop(1, 1, c)
    plan_block(1)
    for c in low:
        hop(1, -1, c)
    plan_block(2)
    plan_block(3)
    dn[0] = jnp.sum(dparts[...].T, axis=0, keepdims=True)
    for dz in Z_PEERS:
        send(dn.at[0], dnr.at[dz - 1], dn_s, dn_r, dz=dz)
    for n in range(PARTS // 2):
        hop(1, 1, low[n])
        hop(1, -1, high[n])
    target_rows(0)
    for n in range(PARTS // 2):
        hop(2, 1, high[n])
        hop(2, -1, low[n])
    target_rows(1)
    for n in range(PARTS // 2):
        hop(2, 1, low[n])
        hop(2, -1, high[n])
    for n in range(PARTS):
        hop(3, 1, (high + low)[n])
        hop(3, -1, (low + high)[n])
    for b in range(2):
        for dy in (1, 3, 2):
            pass_on(dy, b)
    mine = pltpu.make_async_copy(tout.at[half], timg_out.at[half], out_sem.at[0])
    mine.start()

    wait(dnr, dn_r)
    first = ORDER.index(0) * OWN
    denom = dn[0, :, first : first + OWN]
    for dz in Z_PEERS:
        first = ORDER.index(dz) * OWN
        denom = denom + dnr[dz - 1, :, first : first + OWN]
    inverse = 1.0 / to_column(jnp.concatenate([denom, denom], axis=1))[:OWN]
    for c in high + low:
        rows = slice(c * STEP, (c + 1) * STEP)
        wait(plus.at[3, c], plus_r.at[3, c])
        wait(minus.at[3, c], minus_r.at[3, c])
        whole = num[ORDER.index(0), rows, :] + plus[3, c] + minus[3, c]
        simg[rows, :] = whole * inverse[rows, :1]
    sources = pltpu.make_async_copy(simg, simg_out, out_sem.at[1])
    sources.start()
    wait(tout.at[other], tb_r)
    swapped = pltpu.make_async_copy(tout.at[other], timg_out.at[other], out_sem.at[2])
    swapped.start()

    wait(auxr, aux_s)
    for dx in (1, 3):
        wait(trecv.at[dx - 1, half], pf_s.at[dx - 1])
    wait(trecv.at[1, near], pfn_s)
    wait(trecv.at[1, far], pff_s)
    for dx in X_PEERS:
        wait(trecv.at[dx - 1, half], sib_s.at[dx - 1])
    for it in range(2):
        wait(lfx.at[it], fx_s.at[it])
        wait(lfz.at[it], fz_s.at[it])
    wait(lgr, gr_s)
    wait(lgw.at[0], gw1_s)
    wait(lgw.at[pl.ds(0, len(WIDE_PEERS) - 1)], gw_s)
    for b in range(2):
        wait(tsib.at[pl.ds(b * 128, 128)], ts_s.at[b])
        wait(ty.at[:, pl.ds(b * 32, 32)], ty_s.at[b])
    wait(ty, ta_s)
    wait(tout.at[half], tb_s)
    wait(dnr, dn_s)
    for s in range(4):
        for c in range(PARTS):
            if s > 0 or c in low:
                wait(plus.at[s, c], plus_s.at[s, c])
            if s > 0 or c in high:
                wait(minus.at[s, c], minus_s.at[s, c])
    mine.wait()
    sources.wait()
    swapped.wait()


def hand_over(simg, timg, simg_out, timg_out, rows, parts, sem):
    count = parts.shape[0]
    size = NJ // count
    pairs = [(simg, rows, simg_out)] + [
        (timg.at[pl.ds(n * size, size)], parts.at[n], timg_out.at[pl.ds(n * size, size)]) for n in range(count)
    ]
    loads = [pltpu.make_async_copy(a, b, sem.at[0, n]) for n, (a, b, _) in enumerate(pairs)]
    stores = [pltpu.make_async_copy(b, c, sem.at[1, n]) for n, (_, b, c) in enumerate(pairs)]
    for load in loads:
        load.start()
    for load, store in zip(loads, stores):
        load.wait()
        store.start()
    for store in stores:
        store.wait()


def on_device(source, target, log_source_mass, log_target_mass):
    dma, vmem = pltpu.SemaphoreType.DMA, pltpu.VMEM
    scratch = [
        vmem((OWN, D), F32),
        dma((3,)),
        vmem((NI, D), BF16),
        vmem((NJ, D), BF16),
        vmem((1, NI), F32),
        vmem((1, NJ), F32),
        dma((7,)),
        vmem((NJ, NI), F32),
        vmem((NZ * OWN, NX * NJ), F32),
        vmem((NX * NJ, D), BF16),
        vmem((NJ, D), F32),
        vmem((NX - 1, NJ, D), F32),
        vmem((NZ * OWN, D), BF16),
        vmem((32, NI), F32),
        vmem((NJ, 128), F32),
        vmem((NJ, 128), F32),
        vmem((8, NI), F32),
        vmem((NZ, OWN, D), F32),
        vmem((NZ * OWN, 128), F32),
        vmem((16, NX * NJ), F32),
        vmem((NZ * OWN, 128), F32),
        vmem((NZ * OWN, NX * NJ), BF16),
        vmem((2, NJ), F32),
        vmem((NX - 1, 2, NJ), F32),
        vmem((2, 2, 1, NI), F32),
        vmem((2, NX - 1, 1, NI), F32),
        vmem((2, NZ - 1, 1, NI), F32),
        vmem((2, 1, NJ), F32),
        vmem((len(ROW_PEERS), 1, NJ), F32),
        vmem((len(WIDE_PEERS), 1, NJ), F32),
        vmem((NI, 128), F32),
        vmem((NJ, D), F32),
        vmem((HALF, D), F32),
        vmem((HALF, D), F32),
        vmem((NY - 1, QUART, D), F32),
        vmem((NJ, D), F32),
        vmem((4, PARTS, STEP, D), F32),
        vmem((4, PARTS, STEP, D), F32),
        vmem((1, 1, NJ), F32),
        vmem((NZ - 1, 1, NJ), F32),
        dma((3,)), dma((3,)), dma, dma, dma, dma, dma, dma,
        dma((3,)), dma((3,)), dma, dma,
        dma((2,)), dma((2,)), dma((2,)), dma((2,)),
        dma, dma, dma, dma,
        dma((2,)), dma((2,)), dma((2,)), dma((3, 2)), dma, dma((3, 2)), dma, dma,
        dma((4, PARTS)), dma((4, PARTS)), dma((4, PARTS)), dma((4, PARTS)), dma, dma,
    ]
    images = pl.pallas_call(
        kernel,
        out_shape=(jax.ShapeDtypeStruct((OWN, D), F32), jax.ShapeDtypeStruct((NJ, D), F32)),
        in_specs=[pl.BlockSpec(memory_space=pl.ANY)] * 4,
        out_specs=(pl.BlockSpec(memory_space=pl.ANY),) * 2,
        scratch_shapes=scratch,
        compiler_params=pltpu.CompilerParams(
            collective_id=0, has_side_effects=True, vmem_limit_bytes=56 * 2**20
        ),
        cost_estimate=pl.CostEstimate(flops=8 * NI * NJ * D, bytes_accessed=4 * 2**20, transcendentals=7 * NI * NJ),
        name="sinkhorn",
    )(source, target, log_source_mass.reshape(1, NI), log_target_mass.reshape(1, NJ))
    return pl.pallas_call(
        hand_over,
        out_shape=(jax.ShapeDtypeStruct((OWN, D), F32), jax.ShapeDtypeStruct((NJ, D), F32)),
        in_specs=[pl.BlockSpec(memory_space=pl.ANY)] * 2,
        out_specs=(pl.BlockSpec(memory_space=pl.ANY),) * 2,
        scratch_shapes=[vmem((OWN, D), F32), vmem((4, NJ // 4, D), F32), dma((2, 4+1))],
        name="hand_over",
    )(*images)


def solution(mesh):
    in_specs = (P("row", None), P("col", None), P("row"), P("col"))
    out_specs = (P(("row", "col"), None), P("col", None))
    return jax.shard_map(
        on_device, mesh=mesh, in_specs=in_specs, out_specs=out_specs, check_vma=False
    )
```

```python
import functools
import math

import jax
import jax.numpy as jnp
from jax import lax
from jax.experimental import pallas as pl
from jax.experimental.pallas import tpu as pltpu
from jax.sharding import PartitionSpec as P

D = 512
NI = 2048
NJ = 512
NY, NK, NZ, NX = 4, 2, 8, 4
OWN = NI // (NZ * NX)
HALF = NJ // NK
QUART = HALF // NY
BLUR = 0.1
LOG2E = math.log2(math.e)
NORM = LOG2E / (D * BLUR)
MESH = pl.DeviceIdType.MESH
F32 = jnp.float32
BF16 = jnp.bfloat16

STEP = 16
PARTS = OWN // STEP
ORDER = [4, 3, 5, 2, 6, 1, 7, 0]
X_PEERS = [1, 2, 3]
Y_PEERS = [2, 1, 3]
Z_PEERS = [4, 3, 5, 2, 6, 1, 7]
ROW_PEERS = [(dy, dk) for dy in (2, 1, 3, 0) for dk in (1, 0) if (dy, dk) != (0, 0)]
WIDE_PEERS = [
    (dy, dk, dx) for dy in (2, 1, 3, 0) for dx in (2, 1, 3, 0) for dk in (1, 0) if (dy, dk, dx) != (0, 0, 0)
]


BARRIER_PEERS = (
    [(0, 0, dz, 0) for dz in Z_PEERS] + [(dy, dk, 0, 0) for dy, dk in ROW_PEERS] + [(0, 0, 0, dx) for dx in X_PEERS]
)


def log2(x):
    return jnp.log(x) * LOG2E


def merge(parts):
    peak = functools.reduce(jnp.maximum, parts)
    return peak + log2(sum(jnp.exp2(part - peak) for part in parts))


def merge_rows(x):
    peak = jnp.max(x, axis=0, keepdims=True)
    return peak + log2(jnp.sum(jnp.exp2(x - peak), axis=0, keepdims=True))


def to_column(row):
    return jnp.broadcast_to(row, (128, row.shape[1])).T


def to_columns(rows):
    rows = rows + [jnp.zeros((128 - len(rows), rows[0].shape[1]), F32)]
    return jnp.concatenate(rows, axis=0).T


def nt_dot(a, b):
    return lax.dot_general(a, b, (((1,), (1,)), ((), ())), preferred_element_type=F32)


def squared_norms(x):
    sq = x.astype(F32)
    sq = sq * sq
    high = sq.astype(BF16)
    low = (sq - high.astype(F32)).astype(BF16)
    ones = jnp.ones((8, D), BF16)
    return (nt_dot(ones, high) + nt_dot(ones, low))[:1]


def kernel(
    src_in, tgt_in, lsm_in, ltm_in, simg_out, timg_out,
    simg, out_sem,    src, tgt, lsm, ltm, in_sem,
    xt, x2, t4, tf, trecv, own, fparts, gparts, acol, browb, num, dparts, arowb, brown, weights,
    aux, auxr, lf, lfx, lfz, lg, lgr, lgw, bcol,
    tn, tsib, tc, ty, tout, plus, minus, dn, dnr,
    pf_s, pf_r, pfn_s, pfn_r, pff_s, pff_r, gw1_s, gw1_r, sib_s, sib_r, aux_s, aux_r, fx_s, fx_r, fz_s, fz_r, gr_s, gr_r, gw_s, gw_r,
    ts_s, ts_r, ty_s, ty_r, ta_s, ta_r, tb_s, tb_r, plus_s, plus_r, minus_s, minus_r, dn_s, dn_r,
):
    row, col = lax.axis_index("row"), lax.axis_index("col")
    y, k, z, x = row // NK, row % NK, col // NX, col % NX

    def dev(dy=0, dk=0, dz=0, dx=0):
        return {
            "row": lax.rem(y + dy, NY) * NK + lax.rem(k + dk, NK),
            "col": lax.rem(z + dz, NZ) * NX + lax.rem(x + dx, NX),
        }

    def send(source, target, send_sem, recv_sem, **to):
        copy = pltpu.make_async_remote_copy(
            source, target, send_sem, recv_sem, device_id=dev(**to), device_id_type=MESH
        )
        copy.start()

    def theirs(dz):
        return pl.ds(pl.multiple_of((lax.rem(z + dz, NZ) * NX + x) * OWN, OWN), OWN)

    def wait(ref, sem):
        pltpu.make_async_copy(ref, ref, sem).wait()

    barrier = pltpu.get_barrier_semaphore()
    for peer in BARRIER_PEERS:
        pl.semaphore_signal(barrier, 1, device_id=dev(*peer), device_id_type=MESH)
    loads = [
        pltpu.make_async_copy(ref, held, in_sem.at[n])
        for n, (ref, held) in enumerate(((tgt_in, tgt), (ltm_in, ltm), (lsm_in, lsm)))
    ] + [
        pltpu.make_async_copy(
            src_in.at[pl.ds(c * 512, 512)], src.at[pl.ds(c * 512, 512)], in_sem.at[3 + c]
        )
        for c in range(4)
    ]
    for load in loads:
        load.start()
    for load in loads[:3]:
        load.wait()

    ls2 = lsm[...] * LOG2E
    lt2 = ltm[...] * LOG2E
    sqy = squared_norms(tgt[...]) * NORM
    aux[0:1, :] = lt2
    aux[1:2, :] = sqy
    acol[...] = to_column(lt2 - sqy)
    half = pl.ds(pl.multiple_of(k * HALF, HALF), HALF)
    other = pl.ds(pl.multiple_of((1 - k) * HALF, HALF), HALF)
    near = pl.ds(pl.multiple_of(k * HALF, HALF), HALF // 2)
    far = pl.ds(pl.multiple_of(k * HALF + HALF // 2, HALF // 2), HALF // 2)
    def f_tile(t):
        lanes = slice(t * 128, (t + 1) * 128)
        for b in range(4):
            rows = slice(b * 128, (b + 1) * 128)
            scores = (xt[rows, lanes] + acol[rows, :]).reshape(16, 8, 128)
            peak = jnp.max(scores, axis=0)
            total = jnp.sum(jnp.exp2(scores - peak[None]), axis=0)
            fparts[b * 8 : (b + 1) * 8, lanes] = peak + log2(total)

    def f_local(out):
        for t in range(NI // 128):
            f_tile(t)
        out[...] = merge_rows(fparts[...])

    def f_round(it):
        for dx in X_PEERS:
            send(lf.at[it, 0], lfx.at[it, dx - 1], fx_s.at[it], fx_r.at[it], dx=dx)
        if it == 0:
            tf[...] = tgt[...].astype(F32)
            t4[:NJ, :] = tgt[...]
            for n, dz in enumerate(ORDER):
                own[n * OWN : (n + 1) * OWN, :] = src[theirs(dz), :]
        wait(lfx.at[it], fx_r.at[it])
        lf[it, 1] = merge([lf[it, 0]] + [lfx[it, dx - 1] for dx in X_PEERS])
        for dz in Z_PEERS:
            send(lf.at[it, 1], lfz.at[it, dz - 1], fz_s.at[it], fz_r.at[it], dz=dz)

    def f_end(it, sqx):
        wait(lfz.at[it], fz_r.at[it])
        f2 = sqx - merge([lf[it, 1]] + [lfz[it, dz - 1] for dz in Z_PEERS])
        return ls2 + f2 - sqx

    def g_local(out):
        def group(r, carry):
            rows = pl.ds(pl.multiple_of(r * 8, 8), 8)
            tiles = [
                xt[rows, t * 128 : (t + 1) * 128] + browb[:, t * 128 : (t + 1) * 128] for t in range(NI // 128)
            ]
            peak = functools.reduce(jnp.maximum, tiles)
            total = sum(jnp.exp2(tile - peak) for tile in tiles)
            gparts[rows, :] = peak + log2(total)
            return carry

        lax.fori_loop(0, NJ // 8, group, 0, unroll=64)
        out[...] = merge_rows(gparts[...].T)

    def wide_scores(dx):
        block = slice(dx * NJ, (dx + 1) * NJ)
        if dx > 0:
            wait(trecv.at[dx - 1, other], sib_r.at[dx - 1])
            t4[block, :] = trecv[dx - 1].astype(BF16)
        x2[:, block] = nt_dot(own[...], t4[block, :]) * (2 * NORM)

    for c in range(NI // 256):
        if c % 2 == 0:
            loads[3 + c // 2].wait()
        xt[:, c * 256 : (c + 1) * 256] = nt_dot(tgt[...], src[c * 256 : (c + 1) * 256, :]) * (2 * NORM)
        if c > 0:
            f_tile(2 * c - 2)
            f_tile(2 * c - 1)
    f_tile(NI // 128 - 2)
    f_tile(NI // 128 - 1)
    lf[0, 0] = merge_rows(fparts[...])
    pl.semaphore_wait(barrier, len(BARRIER_PEERS))
    f_round(0)
    for dx in X_PEERS:
        send(aux, auxr.at[dx - 1], aux_s, aux_r, dx=dx)
    for dx in (1, 3):
        send(tf.at[half], trecv.at[dx - 1, half], pf_s.at[dx - 1], pf_r.at[dx - 1], dx=dx)
    sqx = jnp.concatenate(
        [squared_norms(src[c * 256 : (c + 1) * 256, :]) for c in range(NI // 256)], axis=1
    ) * NORM
    brow = f_end(0, sqx)
    browb[...] = jnp.broadcast_to(brow, (8, NI))
    g_local(lg.at[0])
    for n, (dy, dk) in enumerate(ROW_PEERS):
        send(lg.at[0], lgr.at[n], gr_s, gr_r, dy=dy, dk=dk)
    wide_scores(0)
    wait(lgr, gr_r)
    g2 = sqy - merge([lg[0]] + [lgr[n] for n in range(len(ROW_PEERS))])
    acol[...] = to_column(lt2 + g2 - sqy)

    f_local(lf.at[1, 0])
    f_round(1)
    for dx in (1, 3):
        wait(trecv.at[dx - 1, half], pf_r.at[dx - 1])
    send(trecv.at[0, near], trecv.at[1, near], pfn_s, pfn_r, dx=1)
    send(trecv.at[2, far], trecv.at[1, far], pff_s, pff_r, dx=3)
    for dx in (1, 3):
        send(trecv.at[dx - 1, half], trecv.at[dx - 1, half], sib_s.at[dx - 1], sib_r.at[dx - 1], dk=1)
    wide_scores(1)
    brow = f_end(1, sqx)
    browb[...] = jnp.broadcast_to(brow, (8, NI))
    g_local(lg.at[1])
    for n, (dy, dk, dx) in enumerate(WIDE_PEERS):
        if (dy, dk, dx) == (0, 1, 0):
            send(lg.at[1], lgw.at[n], gw1_s, gw1_r, dy=dy, dk=dk, dx=dx)
        else:
            send(lg.at[1], lgw.at[n], gw_s, gw_r.at[dx], dy=dy, dk=dk, dx=dx)

    gparts[...] = to_column(lg[1])
    for b in range(4):
        start = ((1 - k) * HALF if b < 2 else k * HALF) + b % 2 * 128
        rows = pl.ds(pl.multiple_of(start, 128), 128)
        shares = jnp.exp2(xt[rows, :] + brow - gparts[rows, :1]).astype(BF16)
        tn[rows, :] = jnp.dot(shares, src[...], preferred_element_type=F32)
        if b < 2:
            send(tn.at[rows], tsib.at[pl.ds(b * 128, 128)], ts_s.at[b], ts_r.at[b], dk=1)

    wait(trecv.at[1, near], pfn_r)
    wait(trecv.at[1, far], pff_r)
    send(trecv.at[1, half], trecv.at[1, half], sib_s.at[1], sib_r.at[1], dk=1)
    bcol[...] = to_column(brow)
    for n, dz in enumerate(ORDER):
        brown[n * OWN : (n + 1) * OWN, :] = bcol[theirs(dz), :]
    wait(lgw.at[0], gw1_r)
    sibling = WIDE_PEERS.index((0, 1, 0))
    pair = merge([lg[1], lgw[sibling]])
    gparts[...] = to_columns([jnp.exp2(lg[1] - pair), jnp.exp2(lgw[sibling] - pair)])
    for b in range(2):
        wait(tsib.at[pl.ds(b * 128, 128)], ts_r.at[b])
        rows = pl.ds(pl.multiple_of(k * HALF + b * 128, 128), 128)
        part = slice(b * 128, (b + 1) * 128)
        tc[part, :] = tn[rows, :] * gparts[rows, :1] + tsib[part, :] * gparts[rows, 1:2]
    for b in range(2):
        for dy in Y_PEERS:
            start = lax.rem(y + dy, NY) * QUART + b * 32
            send(
                tc.at[pl.ds(pl.multiple_of(start, 32), 32)], ty.at[dy - 1, pl.ds(b * 32, 32)],
                ty_s.at[b], ty_r.at[dy - 1, b], dy=dy,
            )

    wide_scores(3)
    wide_scores(2)

    wait(auxr, aux_r)
    arow = {}
    for b in (0, 1, 3, 2):
        wait(lgw.at[pl.ds(0, NY * NK - (2 if b == 0 else 0))], gw_r.at[b])
        parts = {dk + NK * dy: lgw[n] for n, (dy, dk, dx) in enumerate(WIDE_PEERS) if dx == b}
        if b == 0:
            parts[0] = lg[1]
            total = merge(list(parts.values()))
            arow[b] = lt2 + (sqy - total) - sqy
            pairs = [merge([parts[NK * dy], parts[NK * dy + 1]]) for dy in range(NY)]
            gparts[...] = to_columns([jnp.exp2(pair - total) for pair in pairs])
        else:
            mass, norm = auxr[b - 1, 0:1, :], auxr[b - 1, 1:2, :]
            arow[b] = mass + (norm - merge(list(parts.values()))) - norm
        arowb[:, b * NJ : (b + 1) * NJ] = jnp.broadcast_to(arow[b], (16, NJ))

    def plan_rows(r, carry):
        rows = pl.ds(pl.multiple_of(r * 16, 16), 16)
        bias = brown[rows, :]
        denom = None
        for t in range(NX * NJ // 128):
            lanes = slice(t * 128, (t + 1) * 128)
            plan = jnp.exp2(x2[rows, lanes] + bias + arowb[:, lanes])
            denom = plan if denom is None else denom + plan
            weights[rows, lanes] = plan.astype(BF16)
        dparts[rows, :] = denom
        return carry

    def piece(dz, c):
        return num.at[ORDER.index(dz % NZ), pl.ds(c * STEP, STEP)]

    def hop(s, way, c):
        buf, ssem, rsem, to = (plus, plus_s, plus_r, 1) if way == 1 else (minus, minus_s, minus_r, NZ - 1)
        mine = piece(way * (4 - s), c)
        if s > 1 or s == 1 and (way == 1) == (c < PARTS // 2):
            wait(buf.at[s - 1, c], rsem.at[s - 1, c])
            mine[...] = mine[...] + buf[s - 1, c]
        send(mine, buf.at[s, c], ssem.at[s, c], rsem.at[s, c], dz=to)

    low, high = list(range(PARTS // 2)), list(range(PARTS // 2, PARTS))

    def plan_block(b):
        lax.fori_loop(b * 8, (b + 1) * 8, plan_rows, 0, unroll=4)
        sums = jnp.dot(weights[b * 128 : (b + 1) * 128, :], t4[...], preferred_element_type=F32)
        num[2 * b] = sums[:OWN]
        num[2 * b + 1] = sums[OWN:]

    def target_rows(b):
        place = pl.ds(pl.multiple_of(k * HALF + y * QUART + b * 32, 32), 32)
        rows = pl.ds(pl.multiple_of(y * QUART + b * 32, 32), 32)
        shares = gparts[place, :]
        whole = tc[rows, :] * shares[:, :1]
        for dy in Y_PEERS:
            part = ty.at[dy - 1, pl.ds(b * 32, 32)]
            wait(part, ty_r.at[dy - 1, b])
            whole = whole + part[...] * shares[:, dy : dy + 1]
        tout[place, :] = whole
        for dy in Y_PEERS:
            send(tout.at[place], tout.at[place], ta_s, ta_r.at[dy - 1, b], dy=dy)
        send(tout.at[place], tout.at[place], tb_s, tb_r, dk=1)

    def pass_on(dy, b):
        start = k * HALF + lax.rem(y + NY - dy, NY) * QUART + b * 32
        place = pl.ds(pl.multiple_of(start, 32), 32)
        wait(tout.at[place], ta_r.at[dy - 1, b])
        send(tout.at[place], tout.at[place], tb_s, tb_r, dk=1)

    def left(s):
        for c in range(PARTS):
            if s > 0 or c in low:
                wait(plus.at[s, c], plus_s.at[s, c])
            if s > 0 or c in high:
                wait(minus.at[s, c], minus_s.at[s, c])

    plan_block(0)
    for n in range(PARTS // 2):
        hop(0, 1, low[n])
        hop(0, -1, high[n])
    for c in high:
        hop(1, 1, c)
    plan_block(1)
    for c in low:
        hop(1, -1, c)
    plan_block(2)
    plan_block(3)
    dn[0] = jnp.sum(dparts[...].T, axis=0, keepdims=True)
    for dz in Z_PEERS:
        send(dn.at[0], dnr.at[dz - 1], dn_s, dn_r, dz=dz)
    for n in range(PARTS // 2):
        hop(1, 1, low[n])
        hop(1, -1, high[n])
    target_rows(0)
    wait(auxr, aux_s)
    for dx in (1, 3):
        wait(trecv.at[dx - 1, half], pf_s.at[dx - 1])
    wait(trecv.at[1, near], pfn_s)
    wait(trecv.at[1, far], pff_s)
    for dx in X_PEERS:
        wait(trecv.at[dx - 1, half], sib_s.at[dx - 1])
    for it in range(2):
        wait(lfx.at[it], fx_s.at[it])
        wait(lfz.at[it], fz_s.at[it])
    wait(lgr, gr_s)
    wait(lgw.at[0], gw1_s)
    wait(lgw.at[pl.ds(0, len(WIDE_PEERS) - 1)], gw_s)
    for b in range(2):
        wait(tsib.at[pl.ds(b * 128, 128)], ts_s.at[b])
        wait(ty.at[:, pl.ds(b * 32, 32)], ty_s.at[b])
    for n in range(PARTS // 2):
        hop(2, 1, high[n])
        hop(2, -1, low[n])
    target_rows(1)
    for n in range(PARTS // 2):
        hop(2, 1, low[n])
        hop(2, -1, high[n])
    left(0)
    left(1)
    for n in range(PARTS):
        hop(3, 1, (high + low)[n])
        hop(3, -1, (low + high)[n])
    for b in range(2):
        for dy in (1, 3, 2):
            pass_on(dy, b)
    left(2)
    mine = pltpu.make_async_copy(tout.at[half], timg_out.at[half], out_sem.at[0])
    mine.start()

    wait(dnr, dn_r)
    first = ORDER.index(0) * OWN
    denom = dn[0, :, first : first + OWN]
    for dz in Z_PEERS:
        first = ORDER.index(dz) * OWN
        denom = denom + dnr[dz - 1, :, first : first + OWN]
    inverse = 1.0 / to_column(jnp.concatenate([denom, denom], axis=1))[:OWN]
    for c in high + low:
        rows = slice(c * STEP, (c + 1) * STEP)
        wait(plus.at[3, c], plus_r.at[3, c])
        wait(minus.at[3, c], minus_r.at[3, c])
        whole = num[ORDER.index(0), rows, :] + plus[3, c] + minus[3, c]
        simg[rows, :] = whole * inverse[rows, :1]
    sources = pltpu.make_async_copy(simg, simg_out, out_sem.at[1])
    sources.start()
    wait(tout.at[other], tb_r)
    swapped = pltpu.make_async_copy(tout.at[other], timg_out.at[other], out_sem.at[2])
    swapped.start()

    wait(ty, ta_s)
    wait(tout.at[half], tb_s)
    wait(dnr, dn_s)
    left(3)
    mine.wait()
    sources.wait()
    swapped.wait()


def hand_over(simg, timg, simg_out, timg_out, rows, parts, sem):
    count = parts.shape[0]
    size = NJ // count
    pairs = [(simg, rows, simg_out)] + [
        (timg.at[pl.ds(n * size, size)], parts.at[n], timg_out.at[pl.ds(n * size, size)]) for n in range(count)
    ]
    loads = [pltpu.make_async_copy(a, b, sem.at[0, n]) for n, (a, b, _) in enumerate(pairs)]
    stores = [pltpu.make_async_copy(b, c, sem.at[1, n]) for n, (_, b, c) in enumerate(pairs)]
    for load in loads:
        load.start()
    for load, store in zip(loads, stores):
        load.wait()
        store.start()
    for store in stores:
        store.wait()


def on_device(source, target, log_source_mass, log_target_mass):
    dma, vmem = pltpu.SemaphoreType.DMA, pltpu.VMEM
    scratch = [
        vmem((OWN, D), F32),
        dma((3,)),
        vmem((NI, D), BF16),
        vmem((NJ, D), BF16),
        vmem((1, NI), F32),
        vmem((1, NJ), F32),
        dma((7,)),
        vmem((NJ, NI), F32),
        vmem((NZ * OWN, NX * NJ), F32),
        vmem((NX * NJ, D), BF16),
        vmem((NJ, D), F32),
        vmem((NX - 1, NJ, D), F32),
        vmem((NZ * OWN, D), BF16),
        vmem((32, NI), F32),
        vmem((NJ, 128), F32),
        vmem((NJ, 128), F32),
        vmem((8, NI), F32),
        vmem((NZ, OWN, D), F32),
        vmem((NZ * OWN, 128), F32),
        vmem((16, NX * NJ), F32),
        vmem((NZ * OWN, 128), F32),
        vmem((NZ * OWN, NX * NJ), BF16),
        vmem((2, NJ), F32),
        vmem((NX - 1, 2, NJ), F32),
        vmem((2, 2, 1, NI), F32),
        vmem((2, NX - 1, 1, NI), F32),
        vmem((2, NZ - 1, 1, NI), F32),
        vmem((2, 1, NJ), F32),
        vmem((len(ROW_PEERS), 1, NJ), F32),
        vmem((len(WIDE_PEERS), 1, NJ), F32),
        vmem((NI, 128), F32),
        vmem((NJ, D), F32),
        vmem((HALF, D), F32),
        vmem((HALF, D), F32),
        vmem((NY - 1, QUART, D), F32),
        vmem((NJ, D), F32),
        vmem((4, PARTS, STEP, D), F32),
        vmem((4, PARTS, STEP, D), F32),
        vmem((1, 1, NJ), F32),
        vmem((NZ - 1, 1, NJ), F32),
        dma((3,)), dma((3,)), dma, dma, dma, dma, dma, dma,
        dma((3,)), dma((3,)), dma, dma,
        dma((2,)), dma((2,)), dma((2,)), dma((2,)),
        dma, dma, dma, dma((NX,)),
        dma((2,)), dma((2,)), dma((2,)), dma((3, 2)), dma, dma((3, 2)), dma, dma,
        dma((4, PARTS)), dma((4, PARTS)), dma((4, PARTS)), dma((4, PARTS)), dma, dma,
    ]
    images = pl.pallas_call(
        kernel,
        out_shape=(jax.ShapeDtypeStruct((OWN, D), F32), jax.ShapeDtypeStruct((NJ, D), F32)),
        in_specs=[pl.BlockSpec(memory_space=pl.ANY)] * 4,
        out_specs=(pl.BlockSpec(memory_space=pl.ANY),) * 2,
        scratch_shapes=scratch,
        compiler_params=pltpu.CompilerParams(
            collective_id=0, has_side_effects=True, vmem_limit_bytes=56 * 2**20
        ),
        cost_estimate=pl.CostEstimate(flops=8 * NI * NJ * D, bytes_accessed=4 * 2**20, transcendentals=7 * NI * NJ),
        name="sinkhorn",
    )(source, target, log_source_mass.reshape(1, NI), log_target_mass.reshape(1, NJ))
    return pl.pallas_call(
        hand_over,
        out_shape=(jax.ShapeDtypeStruct((OWN, D), F32), jax.ShapeDtypeStruct((NJ, D), F32)),
        in_specs=[pl.BlockSpec(memory_space=pl.ANY)] * 2,
        out_specs=(pl.BlockSpec(memory_space=pl.ANY),) * 2,
        scratch_shapes=[vmem((OWN, D), F32), vmem((4, NJ // 4, D), F32), dma((2, 4+1))],
        name="hand_over",
    )(*images)


def solution(mesh):
    in_specs = (P("row", None), P("col", None), P("row"), P("col"))
    out_specs = (P(("row", "col"), None), P("col", None))
    return jax.shard_map(
        on_device, mesh=mesh, in_specs=in_specs, out_specs=out_specs, check_vma=False
    )
```

```python
import functools
import math

import jax
import jax.numpy as jnp
from jax import lax
from jax.experimental import pallas as pl
from jax.experimental.pallas import tpu as pltpu
from jax.sharding import PartitionSpec as P

D = 512
NI = 2048
NJ = 512
NY, NK, NZ, NX = 4, 2, 8, 4
OWN = NI // (NZ * NX)
HALF = NJ // NK
QUART = HALF // NY
BLUR = 0.1
LOG2E = math.log2(math.e)
NORM = LOG2E / (D * BLUR)
MESH = pl.DeviceIdType.MESH
F32 = jnp.float32
BF16 = jnp.bfloat16

STEP = 16
PARTS = OWN // STEP
ORDER = [4, 3, 5, 2, 6, 1, 7, 0]
X_PEERS = [1, 2, 3]
Y_PEERS = [2, 1, 3]
Z_PEERS = [4, 3, 5, 2, 6, 1, 7]
ROW_PEERS = [(dy, dk) for dy in (2, 1, 3, 0) for dk in (1, 0) if (dy, dk) != (0, 0)]
WIDE_PEERS = [
    (dy, dk, dx) for dy in (2, 1, 3, 0) for dx in (2, 1, 3, 0) for dk in (1, 0) if (dy, dk, dx) != (0, 0, 0)
]


BARRIER_PEERS = (
    [(0, 0, dz, 0) for dz in Z_PEERS] + [(dy, dk, 0, 0) for dy, dk in ROW_PEERS] + [(0, 0, 0, dx) for dx in X_PEERS]
)


def log2(x):
    return jnp.log(x) * LOG2E


def merge(parts):
    peak = functools.reduce(jnp.maximum, parts)
    return peak + log2(sum(jnp.exp2(part - peak) for part in parts))


def merge_rows(x):
    peak = jnp.max(x, axis=0, keepdims=True)
    return peak + log2(jnp.sum(jnp.exp2(x - peak), axis=0, keepdims=True))


def to_column(row):
    return jnp.broadcast_to(row, (128, row.shape[1])).T


def to_columns(rows):
    rows = rows + [jnp.zeros((128 - len(rows), rows[0].shape[1]), F32)]
    return jnp.concatenate(rows, axis=0).T


def nt_dot(a, b):
    return lax.dot_general(a, b, (((1,), (1,)), ((), ())), preferred_element_type=F32)


def squared_norms(x):
    sq = x.astype(F32)
    sq = sq * sq
    high = sq.astype(BF16)
    low = (sq - high.astype(F32)).astype(BF16)
    ones = jnp.ones((8, D), BF16)
    return (nt_dot(ones, high) + nt_dot(ones, low))[:1]


def kernel(
    src_in, tgt_in, lsm_in, ltm_in, simg_out, timg_out,
    simg, out_sem,    src, tgt, lsm, ltm, in_sem,
    xt, x2, t4, tf, trecv, own, fparts, gparts, acol, browb, num, dparts, arowb, brown, weights,
    aux, auxr, lf, lfx, lfz, lg, lgr, lgw, bcol,
    tn, tsib, tc, ty, tout, plus, minus, dn, dnr,
    pf_s, pf_r, pfn_s, pfn_r, pff_s, pff_r, gw1_s, gw1_r, sib_s, sib_r, aux_s, aux_r, fx_s, fx_r, fz_s, fz_r, gr_s, gr_r, gw_s, gw_r,
    ts_s, ts_r, ty_s, ty_r, ta_s, ta_r, tb_s, tb_r, plus_s, plus_r, minus_s, minus_r, dn_s, dn_r,
):
    row, col = lax.axis_index("row"), lax.axis_index("col")
    y, k, z, x = row // NK, row % NK, col // NX, col % NX

    def dev(dy=0, dk=0, dz=0, dx=0):
        return {
            "row": lax.rem(y + dy, NY) * NK + lax.rem(k + dk, NK),
            "col": lax.rem(z + dz, NZ) * NX + lax.rem(x + dx, NX),
        }

    def send(source, target, send_sem, recv_sem, **to):
        copy = pltpu.make_async_remote_copy(
            source, target, send_sem, recv_sem, device_id=dev(**to), device_id_type=MESH
        )
        copy.start()

    def theirs(dz):
        return pl.ds(pl.multiple_of((lax.rem(z + dz, NZ) * NX + x) * OWN, OWN), OWN)

    def wait(ref, sem):
        pltpu.make_async_copy(ref, ref, sem).wait()

    barrier = pltpu.get_barrier_semaphore()
    for peer in BARRIER_PEERS:
        pl.semaphore_signal(barrier, 1, device_id=dev(*peer), device_id_type=MESH)
    loads = [
        pltpu.make_async_copy(ref, held, in_sem.at[n])
        for n, (ref, held) in enumerate(((tgt_in, tgt), (ltm_in, ltm), (lsm_in, lsm)))
    ] + [
        pltpu.make_async_copy(
            src_in.at[pl.ds(c * 512, 512)], src.at[pl.ds(c * 512, 512)], in_sem.at[3 + c]
        )
        for c in range(4)
    ]
    for load in loads:
        load.start()
    for load in loads[:3]:
        load.wait()

    ls2 = lsm[...] * LOG2E
    lt2 = ltm[...] * LOG2E
    sqy = squared_norms(tgt[...]) * NORM
    aux[0:1, :] = lt2
    aux[1:2, :] = sqy
    acol[...] = to_column(lt2 - sqy)
    half = pl.ds(pl.multiple_of(k * HALF, HALF), HALF)
    other = pl.ds(pl.multiple_of((1 - k) * HALF, HALF), HALF)
    near = pl.ds(pl.multiple_of(k * HALF, HALF), HALF // 2)
    far = pl.ds(pl.multiple_of(k * HALF + HALF // 2, HALF // 2), HALF // 2)
    def f_tile(t):
        lanes = slice(t * 128, (t + 1) * 128)
        for b in range(4):
            rows = slice(b * 128, (b + 1) * 128)
            scores = (xt[rows, lanes] + acol[rows, :]).reshape(16, 8, 128)
            peak = jnp.max(scores, axis=0)
            total = jnp.sum(jnp.exp2(scores - peak[None]), axis=0)
            fparts[b * 8 : (b + 1) * 8, lanes] = peak + log2(total)

    def f_local(out):
        for t in range(NI // 128):
            f_tile(t)
        out[...] = merge_rows(fparts[...])

    def f_round(it):
        for dx in X_PEERS:
            send(lf.at[it, 0], lfx.at[it, dx - 1], fx_s.at[it], fx_r.at[it], dx=dx)
        if it == 0:
            tf[...] = tgt[...].astype(F32)
            t4[:NJ, :] = tgt[...]
            for n, dz in enumerate(ORDER):
                own[n * OWN : (n + 1) * OWN, :] = src[theirs(dz), :]
        wait(lfx.at[it], fx_r.at[it])
        lf[it, 1] = merge([lf[it, 0]] + [lfx[it, dx - 1] for dx in X_PEERS])
        for dz in Z_PEERS:
            send(lf.at[it, 1], lfz.at[it, dz - 1], fz_s.at[it], fz_r.at[it], dz=dz)

    def f_end(it, sqx):
        wait(lfz.at[it], fz_r.at[it])
        f2 = sqx - merge([lf[it, 1]] + [lfz[it, dz - 1] for dz in Z_PEERS])
        return ls2 + f2 - sqx

    def g_local(out):
        def group(r, carry):
            rows = pl.ds(pl.multiple_of(r * 8, 8), 8)
            tiles = [
                xt[rows, t * 128 : (t + 1) * 128] + browb[:, t * 128 : (t + 1) * 128] for t in range(NI // 128)
            ]
            peak = functools.reduce(jnp.maximum, tiles)
            total = sum(jnp.exp2(tile - peak) for tile in tiles)
            gparts[rows, :] = peak + log2(total)
            return carry

        lax.fori_loop(0, NJ // 8, group, 0, unroll=64)
        out[...] = merge_rows(gparts[...].T)

    def wide_scores(dx):
        block = slice(dx * NJ, (dx + 1) * NJ)
        if dx > 0:
            wait(trecv.at[dx - 1, other], sib_r.at[dx - 1])
            t4[block, :] = trecv[dx - 1].astype(BF16)
        x2[:, block] = nt_dot(own[...], t4[block, :]) * (2 * NORM)

    for c in range(NI // 256):
        if c % 2 == 0:
            loads[3 + c // 2].wait()
        xt[:, c * 256 : (c + 1) * 256] = nt_dot(tgt[...], src[c * 256 : (c + 1) * 256, :]) * (2 * NORM)
        if c > 0:
            f_tile(2 * c - 2)
            f_tile(2 * c - 1)
    f_tile(NI // 128 - 2)
    f_tile(NI // 128 - 1)
    lf[0, 0] = merge_rows(fparts[...])
    pl.semaphore_wait(barrier, len(BARRIER_PEERS))
    f_round(0)
    for dx in X_PEERS:
        send(aux, auxr.at[dx - 1], aux_s, aux_r, dx=dx)
    for dx in (1, 3):
        send(tf.at[half], trecv.at[dx - 1, half], pf_s.at[dx - 1], pf_r.at[dx - 1], dx=dx)
    sqx = jnp.concatenate(
        [squared_norms(src[c * 256 : (c + 1) * 256, :]) for c in range(NI // 256)], axis=1
    ) * NORM
    brow = f_end(0, sqx)
    browb[...] = jnp.broadcast_to(brow, (8, NI))
    g_local(lg.at[0])
    for n, (dy, dk) in enumerate(ROW_PEERS):
        send(lg.at[0], lgr.at[n], gr_s, gr_r, dy=dy, dk=dk)
    wide_scores(0)
    wait(lgr, gr_r)
    g2 = sqy - merge([lg[0]] + [lgr[n] for n in range(len(ROW_PEERS))])
    acol[...] = to_column(lt2 + g2 - sqy)

    f_local(lf.at[1, 0])
    f_round(1)
    for dx in (1, 3):
        wait(trecv.at[dx - 1, half], pf_r.at[dx - 1])
    send(trecv.at[0, near], trecv.at[1, near], pfn_s, pfn_r, dx=1)
    send(trecv.at[2, far], trecv.at[1, far], pff_s, pff_r, dx=3)
    for dx in (1, 3):
        send(trecv.at[dx - 1, half], trecv.at[dx - 1, half], sib_s.at[dx - 1], sib_r.at[dx - 1], dk=1)
    wide_scores(1)
    brow = f_end(1, sqx)
    browb[...] = jnp.broadcast_to(brow, (8, NI))
    g_local(lg.at[1])
    for n, (dy, dk, dx) in enumerate(WIDE_PEERS):
        if (dy, dk, dx) == (0, 1, 0):
            send(lg.at[1], lgw.at[n], gw1_s, gw1_r, dy=dy, dk=dk, dx=dx)
        else:
            send(lg.at[1], lgw.at[n], gw_s, gw_r.at[dx], dy=dy, dk=dk, dx=dx)

    gparts[...] = to_column(lg[1])
    for b in range(4):
        start = ((1 - k) * HALF if b < 2 else k * HALF) + b % 2 * 128
        rows = pl.ds(pl.multiple_of(start, 128), 128)
        shares = jnp.exp2(xt[rows, :] + brow - gparts[rows, :1]).astype(BF16)
        tn[rows, :] = jnp.dot(shares, src[...], preferred_element_type=F32)
        if b < 2:
            send(tn.at[rows], tsib.at[pl.ds(b * 128, 128)], ts_s.at[b], ts_r.at[b], dk=1)

    wait(trecv.at[1, near], pfn_r)
    wait(trecv.at[1, far], pff_r)
    send(trecv.at[1, half], trecv.at[1, half], sib_s.at[1], sib_r.at[1], dk=1)
    bcol[...] = to_column(brow)
    for n, dz in enumerate(ORDER):
        brown[n * OWN : (n + 1) * OWN, :] = bcol[theirs(dz), :]
    wait(lgw.at[0], gw1_r)
    sibling = WIDE_PEERS.index((0, 1, 0))
    pair = merge([lg[1], lgw[sibling]])
    gparts[...] = to_columns([jnp.exp2(lg[1] - pair), jnp.exp2(lgw[sibling] - pair)])
    for b in range(2):
        wait(tsib.at[pl.ds(b * 128, 128)], ts_r.at[b])
        rows = pl.ds(pl.multiple_of(k * HALF + b * 128, 128), 128)
        part = slice(b * 128, (b + 1) * 128)
        tc[part, :] = tn[rows, :] * gparts[rows, :1] + tsib[part, :] * gparts[rows, 1:2]
    for b in range(2):
        for dy in Y_PEERS:
            start = lax.rem(y + dy, NY) * QUART + b * 32
            send(
                tc.at[pl.ds(pl.multiple_of(start, 32), 32)], ty.at[dy - 1, pl.ds(b * 32, 32)],
                ty_s.at[b], ty_r.at[dy - 1, b], dy=dy,
            )

    wide_scores(3)
    wide_scores(2)

    wait(auxr, aux_r)
    arow = {}
    for b in (0, 1, 3, 2):
        wait(lgw.at[pl.ds(0, NY * NK - (2 if b == 0 else 0))], gw_r.at[b])
        parts = {dk + NK * dy: lgw[n] for n, (dy, dk, dx) in enumerate(WIDE_PEERS) if dx == b}
        if b == 0:
            parts[0] = lg[1]
            total = merge(list(parts.values()))
            arow[b] = lt2 + (sqy - total) - sqy
            pairs = [merge([parts[NK * dy], parts[NK * dy + 1]]) for dy in range(NY)]
            gparts[...] = to_columns([jnp.exp2(pair - total) for pair in pairs])
        else:
            mass, norm = auxr[b - 1, 0:1, :], auxr[b - 1, 1:2, :]
            arow[b] = mass + (norm - merge(list(parts.values()))) - norm
        arowb[:, b * NJ : (b + 1) * NJ] = jnp.broadcast_to(arow[b], (16, NJ))

    def plan_rows(r, carry):
        rows = pl.ds(pl.multiple_of(r * 16, 16), 16)
        bias = brown[rows, :]
        denom = None
        for t in range(NX * NJ // 128):
            lanes = slice(t * 128, (t + 1) * 128)
            plan = jnp.exp2(x2[rows, lanes] + bias + arowb[:, lanes])
            denom = plan if denom is None else denom + plan
            weights[rows, lanes] = plan.astype(BF16)
        dparts[rows, :] = denom
        return carry

    def piece(dz, c):
        return num.at[ORDER.index(dz % NZ), pl.ds(c * STEP, STEP)]

    def hop(s, way, c):
        buf, ssem, rsem, to = (plus, plus_s, plus_r, 1) if way == 1 else (minus, minus_s, minus_r, NZ - 1)
        mine = piece(way * (4 - s), c)
        if s > 1 or s == 1 and (way == 1) == (c < PARTS // 2):
            wait(buf.at[s - 1, c], rsem.at[s - 1, c])
            mine[...] = mine[...] + buf[s - 1, c]
        send(mine, buf.at[s, c], ssem.at[s, c], rsem.at[s, c], dz=to)

    low, high = list(range(PARTS // 2)), list(range(PARTS // 2, PARTS))

    def plan_block(b):
        lax.fori_loop(b * 8, (b + 1) * 8, plan_rows, 0, unroll=4)
        sums = jnp.dot(weights[b * 128 : (b + 1) * 128, :], t4[...], preferred_element_type=F32)
        num[2 * b] = sums[:OWN]
        num[2 * b + 1] = sums[OWN:]

    def target_rows(b):
        place = pl.ds(pl.multiple_of(k * HALF + y * QUART + b * 32, 32), 32)
        rows = pl.ds(pl.multiple_of(y * QUART + b * 32, 32), 32)
        shares = gparts[place, :]
        whole = tc[rows, :] * shares[:, :1]
        for dy in Y_PEERS:
            part = ty.at[dy - 1, pl.ds(b * 32, 32)]
            wait(part, ty_r.at[dy - 1, b])
            whole = whole + part[...] * shares[:, dy : dy + 1]
        tout[place, :] = whole
        for dy in Y_PEERS:
            send(tout.at[place], tout.at[place], ta_s, ta_r.at[dy - 1, b], dy=dy)
        send(tout.at[place], tout.at[place], tb_s, tb_r, dk=1)

    def pass_on(dy, b):
        start = k * HALF + lax.rem(y + NY - dy, NY) * QUART + b * 32
        place = pl.ds(pl.multiple_of(start, 32), 32)
        wait(tout.at[place], ta_r.at[dy - 1, b])
        send(tout.at[place], tout.at[place], tb_s, tb_r, dk=1)

    def left(s):
        for c in range(PARTS):
            if s > 0 or c in low:
                wait(plus.at[s, c], plus_s.at[s, c])
            if s > 0 or c in high:
                wait(minus.at[s, c], minus_s.at[s, c])

    plan_block(0)
    for n in range(PARTS // 2):
        hop(0, 1, low[n])
        hop(0, -1, high[n])
    for c in high:
        hop(1, 1, c)
    plan_block(1)
    for c in low:
        hop(1, -1, c)
    plan_block(2)
    plan_block(3)
    dn[0] = jnp.sum(dparts[...].T, axis=0, keepdims=True)
    for dz in Z_PEERS:
        send(dn.at[0], dnr.at[dz - 1], dn_s, dn_r, dz=dz)
    for n in range(PARTS // 2):
        hop(1, 1, low[n])
        hop(1, -1, high[n])
    target_rows(0)
    target_rows(1)
    wait(auxr, aux_s)
    for dx in (1, 3):
        wait(trecv.at[dx - 1, half], pf_s.at[dx - 1])
    wait(trecv.at[1, near], pfn_s)
    wait(trecv.at[1, far], pff_s)
    for dx in X_PEERS:
        wait(trecv.at[dx - 1, half], sib_s.at[dx - 1])
    for it in range(2):
        wait(lfx.at[it], fx_s.at[it])
        wait(lfz.at[it], fz_s.at[it])
    wait(lgr, gr_s)
    wait(lgw.at[0], gw1_s)
    wait(lgw.at[pl.ds(0, len(WIDE_PEERS) - 1)], gw_s)
    for b in range(2):
        wait(tsib.at[pl.ds(b * 128, 128)], ts_s.at[b])
        wait(ty.at[:, pl.ds(b * 32, 32)], ty_s.at[b])
    for n in range(PARTS // 2):
        hop(2, 1, high[n])
        hop(2, -1, low[n])
    for n in range(PARTS // 2):
        hop(2, 1, low[n])
        hop(2, -1, high[n])
    left(0)
    left(1)
    for n in range(PARTS):
        hop(3, 1, (high + low)[n])
        hop(3, -1, (low + high)[n])
    for b in range(2):
        for dy in (1, 3, 2):
            pass_on(dy, b)
    left(2)
    mine = pltpu.make_async_copy(tout.at[half], timg_out.at[half], out_sem.at[0])
    mine.start()

    wait(dnr, dn_r)
    first = ORDER.index(0) * OWN
    denom = dn[0, :, first : first + OWN]
    for dz in Z_PEERS:
        first = ORDER.index(dz) * OWN
        denom = denom + dnr[dz - 1, :, first : first + OWN]
    inverse = 1.0 / to_column(jnp.concatenate([denom, denom], axis=1))[:OWN]
    for c in high + low:
        rows = slice(c * STEP, (c + 1) * STEP)
        wait(plus.at[3, c], plus_r.at[3, c])
        wait(minus.at[3, c], minus_r.at[3, c])
        whole = num[ORDER.index(0), rows, :] + plus[3, c] + minus[3, c]
        simg[rows, :] = whole * inverse[rows, :1]
    sources = pltpu.make_async_copy(simg, simg_out, out_sem.at[1])
    sources.start()
    wait(tout.at[other], tb_r)
    swapped = pltpu.make_async_copy(tout.at[other], timg_out.at[other], out_sem.at[2])
    swapped.start()

    wait(ty, ta_s)
    wait(tout.at[half], tb_s)
    wait(dnr, dn_s)
    left(3)
    mine.wait()
    sources.wait()
    swapped.wait()


def hand_over(simg, timg, simg_out, timg_out, rows, parts, sem):
    count = parts.shape[0]
    size = NJ // count
    pairs = [(simg, rows, simg_out)] + [
        (timg.at[pl.ds(n * size, size)], parts.at[n], timg_out.at[pl.ds(n * size, size)]) for n in range(count)
    ]
    loads = [pltpu.make_async_copy(a, b, sem.at[0, n]) for n, (a, b, _) in enumerate(pairs)]
    stores = [pltpu.make_async_copy(b, c, sem.at[1, n]) for n, (_, b, c) in enumerate(pairs)]
    for load in loads:
        load.start()
    for load, store in zip(loads, stores):
        load.wait()
        store.start()
    for store in stores:
        store.wait()


def on_device(source, target, log_source_mass, log_target_mass):
    dma, vmem = pltpu.SemaphoreType.DMA, pltpu.VMEM
    scratch = [
        vmem((OWN, D), F32),
        dma((3,)),
        vmem((NI, D), BF16),
        vmem((NJ, D), BF16),
        vmem((1, NI), F32),
        vmem((1, NJ), F32),
        dma((7,)),
        vmem((NJ, NI), F32),
        vmem((NZ * OWN, NX * NJ), F32),
        vmem((NX * NJ, D), BF16),
        vmem((NJ, D), F32),
        vmem((NX - 1, NJ, D), F32),
        vmem((NZ * OWN, D), BF16),
        vmem((32, NI), F32),
        vmem((NJ, 128), F32),
        vmem((NJ, 128), F32),
        vmem((8, NI), F32),
        vmem((NZ, OWN, D), F32),
        vmem((NZ * OWN, 128), F32),
        vmem((16, NX * NJ), F32),
        vmem((NZ * OWN, 128), F32),
        vmem((NZ * OWN, NX * NJ), BF16),
        vmem((2, NJ), F32),
        vmem((NX - 1, 2, NJ), F32),
        vmem((2, 2, 1, NI), F32),
        vmem((2, NX - 1, 1, NI), F32),
        vmem((2, NZ - 1, 1, NI), F32),
        vmem((2, 1, NJ), F32),
        vmem((len(ROW_PEERS), 1, NJ), F32),
        vmem((len(WIDE_PEERS), 1, NJ), F32),
        vmem((NI, 128), F32),
        vmem((NJ, D), F32),
        vmem((HALF, D), F32),
        vmem((HALF, D), F32),
        vmem((NY - 1, QUART, D), F32),
        vmem((NJ, D), F32),
        vmem((4, PARTS, STEP, D), F32),
        vmem((4, PARTS, STEP, D), F32),
        vmem((1, 1, NJ), F32),
        vmem((NZ - 1, 1, NJ), F32),
        dma((3,)), dma((3,)), dma, dma, dma, dma, dma, dma,
        dma((3,)), dma((3,)), dma, dma,
        dma((2,)), dma((2,)), dma((2,)), dma((2,)),
        dma, dma, dma, dma((NX,)),
        dma((2,)), dma((2,)), dma((2,)), dma((3, 2)), dma, dma((3, 2)), dma, dma,
        dma((4, PARTS)), dma((4, PARTS)), dma((4, PARTS)), dma((4, PARTS)), dma, dma,
    ]
    images = pl.pallas_call(
        kernel,
        out_shape=(jax.ShapeDtypeStruct((OWN, D), F32), jax.ShapeDtypeStruct((NJ, D), F32)),
        in_specs=[pl.BlockSpec(memory_space=pl.ANY)] * 4,
        out_specs=(pl.BlockSpec(memory_space=pl.ANY),) * 2,
        scratch_shapes=scratch,
        compiler_params=pltpu.CompilerParams(
            collective_id=0, has_side_effects=True, vmem_limit_bytes=56 * 2**20
        ),
        cost_estimate=pl.CostEstimate(flops=8 * NI * NJ * D, bytes_accessed=4 * 2**20, transcendentals=7 * NI * NJ),
        name="sinkhorn",
    )(source, target, log_source_mass.reshape(1, NI), log_target_mass.reshape(1, NJ))
    return pl.pallas_call(
        hand_over,
        out_shape=(jax.ShapeDtypeStruct((OWN, D), F32), jax.ShapeDtypeStruct((NJ, D), F32)),
        in_specs=[pl.BlockSpec(memory_space=pl.ANY)] * 2,
        out_specs=(pl.BlockSpec(memory_space=pl.ANY),) * 2,
        scratch_shapes=[vmem((OWN, D), F32), vmem((4, NJ // 4, D), F32), dma((2, 4+1))],
        name="hand_over",
    )(*images)


def solution(mesh):
    in_specs = (P("row", None), P("col", None), P("row"), P("col"))
    out_specs = (P(("row", "col"), None), P("col", None))
    return jax.shard_map(
        on_device, mesh=mesh, in_specs=in_specs, out_specs=out_specs, check_vma=False
    )
```
